256 devices in a mesh: partner: 32 (over z, x), row: 8 (over y, core).
Axes of the slice: x: 4, y: 4, z: 8, core: 2. Of those that a mesh axis runs over, the one named last changes fastest.
Arguments:
- rhs: float32 [131072, 1024], P(('partner', 'row')), may hold values from -6 to 6
- leaf_inverse: bfloat16 [131072, 4096], P(('partner', 'row')), may hold values from -0.09375 to 0.09375
- leaf_sizes: int32 [32], P('partner'), may hold values from 2048 to 4096, as said below
- u_tilde: bfloat16 [5, 131072, 128], P(None, ('partner', 'row')), may hold values from -0.25 to 0.25
- v_right: bfloat16 [5, 131072, 128], P(None, ('partner', 'row'))
- cap_factor: float32 [5, 32, 128, 128], P(None, 'partner'), as said below
Outputs:
- solution: float32 [131072, 1024], P(('partner', 'row'))
The draws below stay inside these ranges and needn't reach their ends.
Inputs may be any that keep to these rules, and one draw needn't show every extreme that they name: `leaf_sizes`: each leaf size lies in 2048 to 4096; some leaf has exactly 4096 and some exactly 2048. cap_factor[l, p] is the same matrix for all leaves p of one node of level l, that is all p that agree above bit l.
All inputs are finite; a program needn't handle non-finite values.
Results may differ from the reference program's by a relative error of at most 0.0095.
Values may be sent and summed in bfloat16 or wider, within the bound.
No kernel may reach another device: no remote copies, remote signals or barrier semaphores. Data moves between devices by JAX's collectives and lax.ppermute only.
A program may use at most 64 MiB of HBM per device.

```python
import jax
import jax.numpy as jnp
from jax import lax

K = 4096
R = 128
S = 1024
LEVELS = 5
NTOT = 131072
N_PARTNER = 32


def draw_leaf_sizes(key, part):
    key = jax.random.fold_in(key, 5)
    first, second = jax.random.split(key)
    sizes = jax.random.randint(first, (N_PARTNER,), K // 2, K + 1, dtype=jnp.int32)
    order = jax.random.permutation(second, N_PARTNER)
    index = jnp.arange(N_PARTNER, dtype=jnp.int32)
    sizes = jnp.where(index == order[0], K, sizes)
    sizes = jnp.where(index == order[1], K // 2, sizes)
    return sizes.astype(jnp.int32)


def draw_v_right(key, part):
    key = jax.random.fold_in(key, 11)
    level = jnp.arange(LEVELS, dtype=jnp.float32)[:, None, None]
    scale = 1.0 / jnp.sqrt(K * 2.0 ** level)
    values = jax.random.normal(key, (LEVELS, NTOT, R), jnp.float32)
    return (values * scale).astype(jnp.bfloat16)


def draw_cap_factor(key, part):
    key = jax.random.fold_in(key, 17)
    eye = jnp.eye(R, dtype=jnp.float32)
    stacked = []
    for level in range(LEVELS):
        nodes = N_PARTNER // 2 ** (level + 1)
        sub = jax.random.fold_in(key, level)
        noise = jax.random.normal(sub, (nodes, R, R), jnp.float32)
        mats = eye[None] + 0.4 * noise / jnp.sqrt(R * 1.0)
        stacked.append(jnp.repeat(mats, 2 ** (level + 1), axis=0))
    return jnp.stack(stacked, axis=0).astype(jnp.float32)


def level_of(rng, extent, pieces, smallest, largest):
    def one(position, blocks):
        draws = jax.random.uniform(jax.random.fold_in(jax.random.fold_in(rng, 6), position), (blocks,), jnp.float32, smallest / len(pieces), largest / len(pieces))
        return jnp.repeat(jnp.exp(draws), extent[position] // blocks).reshape((-1,) + (1,) * (len(extent) - position - 1))

    factor_of = one(*pieces[0])
    for cut in pieces[1:]:
        factor_of = factor_of * one(*cut)
    return factor_of


def bell_draw(stream_key, shape, deviation, most, cuts=(), kind=jnp.bfloat16):
    drawn = jax.random.normal(stream_key, shape, jnp.float32) * deviation
    if len(cuts) > 0:
        drawn = level_of(stream_key, shape, cuts, -0.22, 0.18) * drawn
    return jnp.clip(drawn, min=-most, max=most).astype(kind)


def setup_inputs(seed: int = 0) -> dict:
    seeds = jax.random.split(jax.random.key(seed), 7)
    return {
        "rhs": bell_draw(seeds[0], (NTOT, S), 1.0, 6.0, ((0, 256),), jnp.float32),
        "leaf_inverse": bell_draw(seeds[1], (NTOT, K), K ** -0.5, 0.09375, ((0, 256),)),
        "leaf_sizes": draw_leaf_sizes(jax.random.fold_in(seeds[6], 71), 0),
        "u_tilde": bell_draw(seeds[3], (LEVELS, NTOT, R), (4 * R) ** -0.5, 0.25, ((1, 256),)),
        "v_right": draw_v_right(jax.random.fold_in(seeds[6], 71), 0),
        "cap_factor": draw_cap_factor(jax.random.fold_in(seeds[6], 71), 0),
    }


def reference(rhs, leaf_inverse, leaf_sizes, u_tilde, v_right, cap_factor):
    highest = lax.Precision.HIGHEST
    parts = N_PARTNER
    local = jnp.arange(K, dtype=jnp.int32)
    live = (local[None, :] < leaf_sizes[:, None]).astype(jnp.float32).reshape(NTOT, 1)
    rhs_b = (rhs * live).astype(jnp.bfloat16).reshape(parts, K, S)
    blocks = leaf_inverse.reshape(parts, K, K)

    def leaf_apply(pair):
        return jnp.dot(pair[0], pair[1], preferred_element_type=jnp.float32)

    solution = lax.map(leaf_apply, (blocks, rhs_b)).reshape(NTOT, S) * live
    basis = u_tilde.astype(jnp.float32) * live[None]
    right = v_right.astype(jnp.float32)
    for level in range(LEVELS):
        span = 2 ** level
        nodes = parts // (2 * span)
        right_l = right[level].reshape(parts, K, R)
        basis_l = basis[level].reshape(parts, K, R)
        proj = jnp.einsum("pkr,pks->prs", right_l, solution.reshape(parts, K, S), precision=highest)
        proj = proj.reshape(nodes, 2, span, R, S).sum(2)
        cap = jnp.einsum("pkr,pkt->prt", right_l, basis_l, precision=highest)
        cap = cap.reshape(nodes, 2, span, R, R).sum(2)
        factor = cap_factor[level, ::2 * span]

        def mult(left, other):
            return jnp.einsum("nij,njk->nik", left, other, precision=highest)

        second = mult(factor, proj[:, 0] - mult(cap[:, 0], proj[:, 1]))
        first = proj[:, 1] - mult(cap[:, 1], second)
        coeff = jnp.stack([first, second], axis=1)
        coeff = jnp.broadcast_to(coeff[:, :, None], (nodes, 2, span, R, S)).reshape(parts, R, S)
        update = jnp.einsum("pkr,prs->pks", basis_l, coeff, precision=highest)
        solution = solution - update.reshape(NTOT, S)
    return solution
```

```python
import jax
import jax.numpy as jnp
from jax import lax
from jax.experimental import pallas as pl
from jax.experimental.pallas import tpu as pltpu
from jax.sharding import PartitionSpec as P

Z, X, Y, C = 8, 4, 4, 2
LEVELS = 5
R = 128
BF = jnp.bfloat16
F32 = jnp.float32
FIRST = (0, 5, 9, 12, 14)
N_CAP = 15
H_FIRST = (0, 4, 7, 9)
N_H = 10
VMEM_LIMIT = 48 * 1024 * 1024


def move(block, where):
    route = []
    for z in range(Z):
        for x in range(X):
            for y in range(Y):
                for c in range(C):
                    z1, x1, y1, c1 = where(z, x, y, c)
                    here = ((z * X + x) * Y + y) * C + c
                    there = ((z1 % Z * X + x1 % X) * Y + y1 % Y) * C + c1 % C
                    route.append((here, there))
    return lax.ppermute(block, ("partner", "row"), route)


def to_core(block):
    return move(block, lambda z, x, y, c: (z, x, y, 1 - c))


def to_y(block, d):
    return move(block, lambda z, x, y, c: (z, x, y + d, c))


def to_x(block, mask):
    return move(block, lambda z, x, y, c: (z, x ^ mask, y, c))


def to_z(block, mask):
    return move(block, lambda z, x, y, c: (z ^ mask, x, y, c))


def dot(a, b):
    return jnp.dot(a, b, preferred_element_type=F32)


def split(a):
    upper = a.astype(BF)
    return upper, (a - upper.astype(F32)).astype(BF)


def dot_16_32(a, b):
    upper, lower = split(b)
    return dot(a, upper) + dot(a, lower)


def dot_32_32(a, b):
    a_upper, a_lower = split(a)
    b_upper, b_lower = split(b)
    return dot(a_upper, b_upper) + (dot(a_upper, b_lower) + dot(a_lower, b_upper))


def kernel_call(body, out_shape, n_scalar, n_in, scratch=(), name=None):
    smem = pl.BlockSpec(memory_space=pltpu.SMEM)
    vmem = pl.BlockSpec(memory_space=pltpu.VMEM)
    outs = out_shape if isinstance(out_shape, (tuple, list)) else (out_shape,)
    out_specs = [vmem] * len(outs)
    return pl.pallas_call(
        body,
        out_shape=out_shape,
        in_specs=[smem] * n_scalar + [vmem] * n_in,
        out_specs=out_specs if isinstance(out_shape, (tuple, list)) else vmem,
        scratch_shapes=list(scratch),
        compiler_params=pltpu.CompilerParams(vmem_limit_bytes=VMEM_LIMIT),
        name=name,
    )


def elimination_body(side_ref, own_ref, sib_ref, g_ref, h_ref):
    rows = lax.broadcasted_iota(jnp.int32, (R, R), 0)
    cols = lax.broadcasted_iota(jnp.int32, (R, R), 1)
    eye = (rows == cols).astype(F32)
    for m in range(LEVELS - 1):
        upper = side_ref[m] == 1
        first = FIRST[m]
        c0 = jnp.where(upper, sib_ref[first], own_ref[first])
        c1 = jnp.where(upper, own_ref[first], sib_ref[first])
        g = g_ref[m]
        g_hi, g_lo = split(g)
        gc0 = dot(g_hi, c0) + dot(g_lo, c0)
        m1 = jnp.where(upper, -gc0, g)
        m0 = jnp.where(upper, eye, 0.0) - dot_16_32(c1, m1)
        m0_hi, m0_lo = split(m0)
        m1_hi, m1_lo = split(m1)
        for l in range(m + 1, LEVELS):
            j = first + l - m
            a0 = jnp.where(upper, sib_ref[j], own_ref[j])
            a1 = jnp.where(upper, own_ref[j], sib_ref[j])
            h = dot(a0, m0_hi) + dot(a0, m0_lo) + dot(a1, m1_hi) + dot(a1, m1_lo)
            hi, lo = split(h)
            at = (H_FIRST[m] + l - m - 1) * R
            h_ref[at : at + R, 0:R] = hi
            h_ref[at : at + R, R : 2 * R] = lo


def project_body(y_ref, va_ref, vb_ref, pa_ref, pb_ref, q_ref):
    y = y_ref[0]
    for block in range(Y):
        rel = lax.rem(block + Y - y, Y)
        at = block * R
        a_hi, a_lo = split(pa_ref[:, at : at + R])
        b_hi, b_lo = split(pb_ref[:, at : at + R])
        q = dot(va_ref[...], jnp.concatenate([a_hi, a_lo], axis=1))
        q = q + dot(vb_ref[...], jnp.concatenate([b_hi, b_lo], axis=1))
        q_ref[rel] = (q[:, :R] + q[:, R:]).astype(BF)


def eliminate_body(q0_ref, q1_ref, q2_ref, q3_ref, h_ref, e_ref):
    q = (q0_ref[...].astype(F32) + q1_ref[...].astype(F32)) + (
        q2_ref[...].astype(F32) + q3_ref[...].astype(F32)
    )
    for m in range(LEVELS):
        e = q[:R].astype(BF)
        e_ref[m * R : (m + 1) * R, :] = e
        if m < LEVELS - 1:
            at, n = H_FIRST[m] * R, (LEVELS - 1 - m) * R
            q = q[R:] - dot(h_ref[at : at + n, :], jnp.concatenate([e, e], axis=0))


def solve(upper, own, sib, cap_own, cap_sib, g):
    s0 = jnp.where(upper, sib, own)
    s1 = jnp.where(upper, own, sib)
    c0 = jnp.where(upper, cap_sib, cap_own)
    c1 = jnp.where(upper, cap_own, cap_sib)
    inner = s0 - dot_16_32(c0, s1)
    t1 = dot_32_32(g, inner)
    t0 = s1 - dot_16_32(c1, t1)
    return jnp.where(upper, t1, t0)


def solve_two_body(levels, side_ref, own_ref, sib_ref, g_ref, a_ref, r1_ref, r2_ref, r3_ref, t_ref):
    low, high = levels
    one = slice(0, R)
    two = slice(R, 2 * R)
    t = solve(
        side_ref[low] == 1,
        a_ref[one].astype(F32),
        r1_ref[one].astype(F32),
        own_ref[FIRST[low]],
        sib_ref[FIRST[low]],
        g_ref[low],
    )
    t_ref[one] = t.astype(BF)
    t = solve(
        side_ref[high] == 1,
        a_ref[two].astype(F32) + r1_ref[two].astype(F32),
        r2_ref[one].astype(F32) + r3_ref[one].astype(F32),
        own_ref[FIRST[high]],
        sib_ref[FIRST[high]],
        g_ref[high],
    )
    t_ref[two] = t.astype(BF)


def solve_last_body(side_ref, own_ref, sib_ref, g_ref, a_ref, r_ref, t_ref):
    last = LEVELS - 1
    t = solve(
        side_ref[last] == 1,
        a_ref[...].astype(F32),
        r_ref[...].astype(F32),
        own_ref[FIRST[last]],
        sib_ref[FIRST[last]],
        g_ref[last],
    )
    t_ref[...] = t.astype(BF)


def finish_body(place_ref, y_own_ref, y_other_ref, u_ref, *refs):
    t_refs, out_ref, t_all = refs[:-2], refs[-2], refs[-1]
    y, c = place_ref[0], place_ref[1]
    half = Y * R
    n = len(t_refs) // 2

    @pl.when(pl.program_id(0) == 0)
    def _():
        for group, core in ((t_refs[:n], c), (t_refs[n:], 1 - c)):
            row = 0
            for ref in group:
                rows = ref.shape[1]
                for k in range(Y):
                    at = core * half + lax.rem(y + k, Y) * R
                    t_all[row : row + rows, pl.ds(pl.multiple_of(at, R), R)] = ref[k]
                row += rows

    for ref, core in ((y_own_ref, c), (y_other_ref, 1 - c)):
        at = pl.ds(pl.multiple_of(core * half, half), half)
        out_ref[:, at] = ref[...] - dot(u_ref[...], t_all[:, at])


def finish(place, y_own, y_other, u, t_own, t_other):
    rows, half = y_own.shape
    tile = min(rows, 128)
    row_block = lambda i, place_ref: (i, 0)
    whole3 = lambda i, place_ref: (0, 0, 0)
    t_all = list(t_own) + list(t_other)
    return pl.pallas_call(
        finish_body,
        out_shape=jax.ShapeDtypeStruct((rows, 2 * half), F32),
        grid_spec=pltpu.PrefetchScalarGridSpec(
            num_scalar_prefetch=1,
            grid=(rows // tile,),
            in_specs=[
                pl.BlockSpec((tile, half), row_block),
                pl.BlockSpec((tile, half), row_block),
                pl.BlockSpec((tile, LEVELS * R), row_block),
            ]
            + [pl.BlockSpec(t.shape, whole3) for t in t_all],
            out_specs=pl.BlockSpec((tile, 2 * half), row_block),
            scratch_shapes=[pltpu.VMEM((LEVELS * R, 2 * half), BF)],
        ),
        compiler_params=pltpu.CompilerParams(vmem_limit_bytes=VMEM_LIMIT),
        name="finish",
    )(place, y_own, y_other, u, *t_all)


def f32(a):
    return a.astype(F32)


def gather_y(block):
    after = to_y(block, -1)
    before = to_y(block, 1)
    far = to_y(block, 2)
    return [block, after, far, before]


def in_place_order(blocks, y):
    twice = jnp.stack(list(blocks) + list(blocks))
    return lax.dynamic_slice_in_dim(twice, lax.rem(Y - y, Y), Y, axis=0)


def capacitances(u, v, y, c):
    local = [
        jnp.einsum("lir,it->lrt", v[m:], u[m], preferred_element_type=F32) for m in range(LEVELS)
    ]
    local = jnp.concatenate(local, axis=0)
    half = R // 2
    mine = lax.dynamic_slice_in_dim(local, c * half, half, axis=1)
    theirs = lax.dynamic_slice_in_dim(local, (1 - c) * half, half, axis=1)
    chip = mine + to_core(theirs)
    part = half // Y
    chip_b = chip.astype(BF)

    def for_y(d):
        return lax.dynamic_slice_in_dim(chip_b, lax.rem(y + d, Y) * part, part, axis=1)

    leaf = lax.dynamic_slice_in_dim(chip, y * part, part, axis=1)
    leaf = leaf + f32(to_y(for_y(1), 1)) + f32(to_y(for_y(2), 2)) + f32(to_y(for_y(3), 3))
    r1 = to_x(leaf, 1)
    r2 = to_x(leaf[FIRST[1] :], 2)
    r3 = to_x(leaf[FIRST[1] :], 3)
    n1 = FIRST[2] - FIRST[1]
    own0, sib0 = leaf[: FIRST[1]], r1[: FIRST[1]]
    own1 = leaf[FIRST[1] : FIRST[2]] + r1[FIRST[1] : FIRST[2]]
    sib1 = r2[:n1] + r3[:n1]
    quad = (leaf[FIRST[2] :] + r1[FIRST[2] :]) + (r2[n1:] + r3[n1:])
    n2 = FIRST[3] - FIRST[2]
    n3 = FIRST[4] - FIRST[3]
    z1 = to_z(quad, 1)
    z2 = to_z(quad[n2:], 2)
    z3 = to_z(quad[n2:], 3)
    own2, sib2 = quad[:n2], z1[:n2]
    own3 = quad[n2 : n2 + n3] + z1[n2 : n2 + n3]
    sib3 = z2[:n3] + z3[:n3]
    own4 = (quad[n2 + n3 :] + z1[n2 + n3 :]) + (z2[n3:] + z3[n3:])
    sib4 = to_z(own4, 4)
    both = jnp.concatenate([own0, own1, own2, own3, own4, sib0, sib1, sib2, sib3, sib4], axis=0)
    by_y = in_place_order(gather_y(both.astype(BF)), y)
    other = to_core(by_y)
    by_core = jnp.stack([jnp.where(c == 0, by_y, other), jnp.where(c == 0, other, by_y)])
    blocks = by_core.transpose(2, 0, 1, 3, 4).reshape(2 * N_CAP, R, R)
    return blocks[:N_CAP], blocks[N_CAP:]


def shards(rhs, leaf_inverse, leaf_sizes, u_tilde, v_right, cap_factor):
    rows, columns = rhs.shape
    half = columns // 2
    row = lax.axis_index("row").astype(jnp.int32)
    partner = lax.axis_index("partner").astype(jnp.int32)
    y, c = row // C, lax.rem(row, C)
    side = (partner >> jnp.arange(LEVELS, dtype=jnp.int32)) & 1
    place = jnp.stack([y, c])
    g = cap_factor[:, 0]

    def live_rows(core):
        at = (y * C + core) * rows + jnp.arange(rows, dtype=jnp.int32)
        return (at < leaf_sizes[0])[:, None]

    live = live_rows(c)
    live_other = live_rows(1 - c)
    rhs_b = jnp.where(live, rhs, 0.0).astype(BF)
    u = jnp.where(live[None], u_tilde, jnp.zeros((), BF))

    mine = lax.dynamic_slice_in_dim(rhs_b, c * half, half, axis=1)
    theirs = to_core(lax.dynamic_slice_in_dim(rhs_b, (1 - c) * half, half, axis=1))
    chip = jnp.concatenate(
        [jnp.where(c == 0, mine, theirs), jnp.where(c == 0, theirs, mine)], axis=0
    )

    a_other = to_core(leaf_inverse)
    v_other = to_core(v_right)
    vt_own = v_right.transpose(0, 2, 1).reshape(LEVELS * R, rows)
    vt_other = v_other.transpose(0, 2, 1).reshape(LEVELS * R, rows)
    u_rows = u.transpose(1, 0, 2).reshape(rows, LEVELS * R)

    def a_block(a, d):
        return lax.dynamic_slice_in_dim(a, lax.rem(y + d, Y) * 2 * rows, 2 * rows, axis=1)

    a_own = [a_block(leaf_inverse, d) for d in range(Y)]
    a_oth = [a_block(a_other, d) for d in range(Y)]

    n_chunks = 2
    width = half // n_chunks
    y_own, y_oth = [], []
    for k in range(n_chunks):
        b0 = chip[:, k * width : (k + 1) * width]
        before = to_y(b0, 1)
        after = to_y(b0, -1)
        far_top = to_y(before[:rows], 1)
        far_bottom = to_y(after[rows:], -1)
        far = jnp.concatenate([far_top, far_bottom], axis=0)
        blocks = (b0, after, far, before)
        for parts, a, alive in ((y_own, a_own, live), (y_oth, a_oth, live_other)):
            total = dot(a[0], blocks[0])
            for d in (3, 1, 2):
                total = total + dot(a[d], blocks[d])
            parts.append(jnp.where(alive, total, 0.0))
    y_own = jnp.concatenate(y_own, axis=1)
    y_oth = jnp.concatenate(y_oth, axis=1)

    cap_own, cap_sib = capacitances(u, v_right, y, c)
    h = kernel_call(
        elimination_body, jax.ShapeDtypeStruct((N_H * R, 2 * R), BF), 1, 3, name="elimination"
    )(side, cap_own, cap_sib, g)

    q = kernel_call(
        project_body, jax.ShapeDtypeStruct((Y, LEVELS * R, R), BF), 1, 4, name="project"
    )(y[None], vt_own, vt_other, y_own, y_oth)
    y_other = to_core(y_oth)

    e = kernel_call(
        eliminate_body, jax.ShapeDtypeStruct((LEVELS * R, R), BF), 0, 5, name="eliminate"
    )(q[0], to_y(q[1], 1), to_y(q[2], 2), to_y(q[3], 3), h)

    two = jax.ShapeDtypeStruct((2 * R, R), BF)
    r1, r2, r3 = to_x(e, 1), to_x(e[R:], 2), to_x(e[R:], 3)
    quad = ((f32(e[2 * R :]) + f32(r1[2 * R :])) + (f32(r2[R:]) + f32(r3[R:]))).astype(BF)
    t01 = kernel_call(
        lambda *refs: solve_two_body((0, 1), *refs), two, 1, 7, name="solve_0_1"
    )(side, cap_own, cap_sib, g, e[: 2 * R], r1[: 2 * R], r2[:R], r3[:R])
    z1, z2, z3 = to_z(quad, 1), to_z(quad[R:], 2), to_z(quad[R:], 3)
    own4 = ((f32(quad[2 * R :]) + f32(z1[2 * R :])) + (f32(z2[R:]) + f32(z3[R:]))).astype(BF)
    t23 = kernel_call(
        lambda *refs: solve_two_body((2, 3), *refs), two, 1, 7, name="solve_2_3"
    )(side, cap_own, cap_sib, g, quad[: 2 * R], z1[: 2 * R], z2[:R], z3[:R])
    sib4 = to_z(own4, 4)
    t4 = kernel_call(
        solve_last_body, jax.ShapeDtypeStruct((R, R), BF), 1, 5, name="solve_4"
    )(side, cap_own, cap_sib, g, own4, sib4)

    t_own = [jnp.stack(gather_y(t01)), jnp.stack(gather_y(jnp.concatenate([t23, t4], axis=0)))]
    t_other = [to_core(t) for t in t_own]
    return finish(place, y_own, y_other, u_rows, t_own, t_other)


def solution(mesh):
    return jax.shard_map(
        shards,
        mesh=mesh,
        in_specs=(
            P(("partner", "row"), None),
            P(("partner", "row"), None),
            P("partner"),
            P(None, ("partner", "row"), None),
            P(None, ("partner", "row"), None),
            P(None, "partner", None, None),
        ),
        out_specs=P(("partner", "row"), None),
        check_vma=False,
    )
```

```python
import jax
import jax.numpy as jnp
from jax import lax
from jax.experimental import pallas as pl
from jax.experimental.pallas import tpu as pltpu
from jax.sharding import PartitionSpec as P

Z, X, Y, C = 8, 4, 4, 2
LEVELS = 5
R = 128
BF = jnp.bfloat16
F32 = jnp.float32
FIRST = (0, 5, 9, 12, 14)
N_CAP = 15
H_FIRST = (0, 4, 7, 9)
N_H = 10
VMEM_LIMIT = 16 * 1024 * 1024
LEAF_VMEM_LIMIT = 52 * 1024 * 1024


def move(block, where):
    route = []
    for z in range(Z):
        for x in range(X):
            for y in range(Y):
                for c in range(C):
                    z1, x1, y1, c1 = where(z, x, y, c)
                    here = ((z * X + x) * Y + y) * C + c
                    there = ((z1 % Z * X + x1 % X) * Y + y1 % Y) * C + c1 % C
                    route.append((here, there))
    return lax.ppermute(block, ("partner", "row"), route)


def after(block, *others):
    return lax.optimization_barrier((block, *others))[0]


def to_core(block):
    return move(block, lambda z, x, y, c: (z, x, y, 1 - c))


def to_y(block, d):
    return move(block, lambda z, x, y, c: (z, x, y + d, c))


def to_x(block, mask):
    return move(block, lambda z, x, y, c: (z, x ^ mask, y, c))


def to_z(block, mask):
    return move(block, lambda z, x, y, c: (z ^ mask, x, y, c))


def dot(a, b):
    return jnp.dot(a, b, preferred_element_type=F32)


def split(a):
    upper = a.astype(BF)
    return upper, (a - upper.astype(F32)).astype(BF)


def dot_16_32(a, b):
    upper, lower = split(b)
    return dot(a, upper) + dot(a, lower)


def dot_32_32(a, b):
    a_upper, a_lower = split(a)
    b_upper, b_lower = split(b)
    return dot(a_upper, b_upper) + (dot(a_upper, b_lower) + dot(a_lower, b_upper))


def kernel_call(body, out_shape, n_scalar, n_in, scratch=(), name=None):
    smem = pl.BlockSpec(memory_space=pltpu.SMEM)
    vmem = pl.BlockSpec(memory_space=pltpu.VMEM)
    outs = out_shape if isinstance(out_shape, (tuple, list)) else (out_shape,)
    out_specs = [vmem] * len(outs)
    return pl.pallas_call(
        body,
        out_shape=out_shape,
        in_specs=[smem] * n_scalar + [vmem] * n_in,
        out_specs=out_specs if isinstance(out_shape, (tuple, list)) else vmem,
        scratch_shapes=list(scratch),
        compiler_params=pltpu.CompilerParams(vmem_limit_bytes=VMEM_LIMIT),
        name=name,
    )


def side_bits(upper, own, sib):
    return jnp.where(upper, sib, own), jnp.where(upper, own, sib)


def live_rhs_body(scalar_ref, rhs_ref, mine_ref, theirs_ref):
    first, c = scalar_ref[0], scalar_ref[1]
    rows, half = mine_ref.shape
    live = first + lax.broadcasted_iota(jnp.int32, (rows, 1), 0) < scalar_ref[2]
    for ref, core in ((mine_ref, c), (theirs_ref, 1 - c)):
        part = rhs_ref[:, pl.ds(pl.multiple_of(core * half, half), half)]
        ref[...] = jnp.where(live, part, 0.0).astype(BF)


def chip_body(scalar_ref, mine_ref, other_ref, chip_ref):
    c = scalar_ref[1]
    rows = mine_ref.shape[0]
    for ref, core in ((mine_ref, c), (other_ref, 1 - c)):
        chip_ref[pl.ds(pl.multiple_of(core * rows, rows), rows), :] = ref[...]


def halves_body(before_ref, behind_ref, top_ref, bottom_ref):
    rows = top_ref.shape[0]
    top_ref[...] = before_ref[:rows]
    bottom_ref[...] = behind_ref[rows:]


def prepare_body(scalar_ref, u_ref, v_ref, u_rows_ref, vt_ref, mine_ref, theirs_ref, cap_ref):
    rows = u_ref.shape[1]
    first, c = scalar_ref[0], scalar_ref[1]
    live = first + lax.broadcasted_iota(jnp.int32, (rows, 1), 0) < scalar_ref[2]
    for l in range(LEVELS):
        u_rows_ref[:, l * R : (l + 1) * R] = jnp.where(live, u_ref[l].astype(F32), 0.0).astype(BF)
        vt_ref[l * R : (l + 1) * R, :] = v_ref[l].T
    for l in range(LEVELS):
        cap = dot(vt_ref[l * R : (l + 1) * R, :], u_rows_ref[:, : (l + 1) * R])
        for m in range(l + 1):
            cap_ref[FIRST[m] + l - m] = cap[:, m * R : (m + 1) * R]
    half = R // 2
    mine_ref[...] = cap_ref[:, pl.ds(pl.multiple_of(c * half, half), half), :]
    theirs_ref[...] = cap_ref[:, pl.ds(pl.multiple_of((1 - c) * half, half), half), :]


def cap_parts_body(scalar_ref, mine_ref, other_ref, own_ref, *send_refs):
    y = scalar_ref[3]
    part = own_ref.shape[1]

    def at(d):
        return pl.ds(pl.multiple_of(((y + d) & (Y - 1)) * part, part), part)

    own_ref[...] = mine_ref[:, at(0), :] + other_ref[:, at(0), :]
    for d, ref in enumerate(send_refs):
        ref[...] = (mine_ref[:, at(d + 1), :] + other_ref[:, at(d + 1), :]).astype(BF)


def cap_leaf_body(own_ref, r1_ref, r2_ref, r3_ref, leaf_ref):
    leaf_ref[...] = (own_ref[...] + r1_ref[...].astype(F32)) + (
        r2_ref[...].astype(F32) + r3_ref[...].astype(F32)
    )


def cap_x_body(leaf_ref, r1_ref, r2_ref, r3_ref, low_ref, quad_ref):
    n0, n1 = FIRST[1], FIRST[2]
    low_ref[0, :n0] = leaf_ref[:n0].astype(BF)
    low_ref[1, :n0] = r1_ref[:n0].astype(BF)
    low_ref[0, n0:] = (leaf_ref[n0:n1] + r1_ref[n0:n1]).astype(BF)
    low_ref[1, n0:] = (r2_ref[n0:n1] + r3_ref[n0:n1]).astype(BF)
    quad_ref[...] = (leaf_ref[n1:] + r1_ref[n1:]) + (r2_ref[n1:] + r3_ref[n1:])


def cap_z_body(quad_ref, z1_ref, z2_ref, z3_ref, mid_ref, last_ref):
    n0, n1 = FIRST[3] - FIRST[2], FIRST[4] - FIRST[2]
    mid_ref[0, :n0] = quad_ref[:n0].astype(BF)
    mid_ref[1, :n0] = z1_ref[:n0].astype(BF)
    mid_ref[0, n0:] = (quad_ref[n0:n1] + z1_ref[n0:n1]).astype(BF)
    mid_ref[1, n0:] = (z2_ref[n0:n1] + z3_ref[n0:n1]).astype(BF)
    last_ref[...] = (quad_ref[n1:] + z1_ref[n1:]) + (z2_ref[n1:] + z3_ref[n1:])


def cap_both_body(low_ref, mid_ref, own4_ref, sib4_ref, both_ref):
    for side, last_ref in enumerate((own4_ref, sib4_ref)):
        at = side * N_CAP
        both_ref[at : at + FIRST[2]] = low_ref[side]
        both_ref[at + FIRST[2] : at + FIRST[4]] = mid_ref[side]
        both_ref[at + FIRST[4]] = last_ref[0].astype(BF)


def cap_stack_body(scalar_ref, b0_ref, b1_ref, b2_ref, b3_ref, out_ref):
    part = b0_ref.shape[1]
    for d, ref in enumerate((b0_ref, b1_ref, b2_ref, b3_ref)):
        at = ((scalar_ref[3] + d) & (Y - 1)) * part
        out_ref[:, pl.ds(pl.multiple_of(at, part), part), :] = ref[...]


def elimination_body(scalar_ref, side_ref, mine_ref, other_ref, g_ref, h_ref, diag_ref, all_ref):
    c = scalar_ref[1]
    half = R // 2
    all_ref[:, pl.ds(pl.multiple_of(c * half, half), half), :] = mine_ref[...]
    all_ref[:, pl.ds(pl.multiple_of((1 - c) * half, half), half), :] = other_ref[...]
    rows = lax.broadcasted_iota(jnp.int32, (R, R), 0)
    cols = lax.broadcasted_iota(jnp.int32, (R, R), 1)
    eye = (rows == cols).astype(F32)
    for m in range(LEVELS):
        upper = side_ref[m] == 1
        first = FIRST[m]
        c0, c1 = side_bits(upper, all_ref[first], all_ref[N_CAP + first])
        diag_ref[m, 0] = c0
        diag_ref[m, 1] = c1
        if m == LEVELS - 1:
            break
        g = g_ref[m]
        g_hi, g_lo = split(g)
        gc0 = dot(g_hi, c0) + dot(g_lo, c0)
        m1 = jnp.where(upper, -gc0, g)
        m0 = jnp.where(upper, eye, 0.0) - dot_16_32(c1, m1)
        m0_hi, m0_lo = split(m0)
        m1_hi, m1_lo = split(m1)
        for l in range(m + 1, LEVELS):
            j = first + l - m
            a0, a1 = side_bits(upper, all_ref[j], all_ref[N_CAP + j])
            h = dot(a0, m0_hi) + dot(a0, m0_lo) + dot(a1, m1_hi) + dot(a1, m1_lo)
            hi, lo = split(h)
            at = (H_FIRST[m] + l - m - 1) * R
            h_ref[at : at + R, 0:R] = hi
            h_ref[at : at + R, R : 2 * R] = lo


def leaf_body(n, final, scalar_ref, a_own_ref, a_oth_ref, *refs):
    refs = list(refs)
    if final:
        blocks, refs = [tuple(refs[:2])], refs[2:]
        sums, (va_ref, vb_ref) = refs[:2], refs[2:4]
        y_refs, q_refs = refs[4:6], refs[6:]
    else:
        blocks, y_refs = [(ref,) for ref in refs[:n]], refs[n:]
        sums = y_refs
    step = pl.program_id(0)
    for k, parts in enumerate(blocks):

        @pl.when(step == k)
        def _(k=k, parts=parts):
            for a_ref, total, y_ref in zip((a_own_ref, a_oth_ref), sums, y_refs):
                depth = a_ref.shape[1] // len(parts)
                new = None
                for j, part in enumerate(parts):
                    term = dot(a_ref[:, j * depth : (j + 1) * depth], part[...])
                    new = term if new is None else new + term
                y_ref[...] = new if k == 0 and not final else total[...] + new

    if final:
        rows = y_refs[0].shape[0]
        y, c, size = scalar_ref[n], scalar_ref[n + 1], scalar_ref[n + 2]
        iota = lax.broadcasted_iota(jnp.int32, (rows, 1), 0)
        for y_ref, core in zip(y_refs, (c, 1 - c)):
            y_ref[...] = jnp.where((y * C + core) * rows + iota < size, y_ref[...], 0.0)
        for d, q_ref in enumerate(q_refs):
            at = pl.ds(pl.multiple_of(((y + d) & (Y - 1)) * R, R), R)
            q = None
            for y_ref, v_ref in zip(y_refs, (va_ref, vb_ref)):
                hi, lo = split(y_ref[:, at])
                new = dot(v_ref[...], jnp.concatenate([hi, lo], axis=1))
                q = new if q is None else q + new
            q_ref[...] = (q[:, :R] + q[:, R:]).astype(BF)


def leaf(scalars, chips, a_own, a_oth, blocks, rest=()):
    rows = a_own.shape[0]
    half = blocks[0].shape[1]
    n = len(chips)
    final = len(rest) > 0
    whole2 = lambda i, scalar_ref: (0, 0)
    a_spec = pl.BlockSpec((rows, C * rows), lambda i, scalar_ref: (0, scalar_ref[i]))
    operands = [*blocks, *rest]
    out_shape = [jax.ShapeDtypeStruct((rows, half), F32)] * 2
    if final:
        out_shape += [jax.ShapeDtypeStruct((LEVELS * R, R), BF)] * Y
    return pl.pallas_call(
        lambda *refs: leaf_body(n, final, *refs),
        out_shape=out_shape,
        grid_spec=pltpu.PrefetchScalarGridSpec(
            num_scalar_prefetch=1,
            grid=(n,),
            in_specs=[a_spec, a_spec] + [pl.BlockSpec(o.shape, whole2) for o in operands],
            out_specs=[pl.BlockSpec(o.shape, whole2) for o in out_shape],
        ),
        compiler_params=pltpu.CompilerParams(vmem_limit_bytes=LEAF_VMEM_LIMIT),
        name="leaf",
    )(jnp.concatenate([jnp.stack(chips), scalars]), a_own, a_oth, *operands)


def eliminate_body(q0_ref, q1_ref, q2_ref, q3_ref, h_ref, e_ref, upper_ref):
    q = (q0_ref[...].astype(F32) + q1_ref[...].astype(F32)) + (
        q2_ref[...].astype(F32) + q3_ref[...].astype(F32)
    )
    for m in range(LEVELS):
        e = q[:R].astype(BF)
        e_ref[m * R : (m + 1) * R, :] = e
        if m > 0:
            upper_ref[(m - 1) * R : m * R, :] = e
        if m < LEVELS - 1:
            at, n = H_FIRST[m] * R, (LEVELS - 1 - m) * R
            q = q[R:] - dot(h_ref[at : at + n, :], jnp.concatenate([e, e], axis=0))


def solve(c0, c1, upper, own, sib, g):
    s0, s1 = side_bits(upper, own, sib)
    inner = s0 - dot_16_32(c0, s1)
    t1 = dot_32_32(g, inner)
    t0 = s1 - dot_16_32(c1, t1)
    return jnp.where(upper, t1, t0)


def solve_two_body(levels, side_ref, diag_ref, g_ref, a_ref, r1_ref, r2_ref, r3_ref, t_ref):
    low, high = levels
    one = slice(0, R)
    two = slice(R, 2 * R)
    t = solve(
        diag_ref[low, 0],
        diag_ref[low, 1],
        side_ref[low] == 1,
        a_ref[one].astype(F32),
        r1_ref[one].astype(F32),
        g_ref[low],
    )
    t_ref[one] = t.astype(BF)
    t = solve(
        diag_ref[high, 0],
        diag_ref[high, 1],
        side_ref[high] == 1,
        a_ref[two].astype(F32) + r1_ref[two].astype(F32),
        r2_ref[one].astype(F32) + r3_ref[one].astype(F32),
        g_ref[high],
    )
    t_ref[two] = t.astype(BF)


def quad_body(e_ref, r1_ref, r2_ref, r3_ref, quad_ref, upper_ref):
    two = slice(2 * R, 5 * R)
    quad = e_ref[two].astype(F32) + r1_ref[two].astype(F32)
    quad = quad + (r2_ref[R:].astype(F32) + r3_ref[R:].astype(F32))
    quad = quad.astype(BF)
    quad_ref[...] = quad
    upper_ref[...] = quad[R:]


def own4_body(quad_ref, z1_ref, z2_ref, z3_ref, own_ref):
    own = quad_ref[2 * R :].astype(F32) + z1_ref[2 * R :].astype(F32)
    own_ref[...] = (own + (z2_ref[R:].astype(F32) + z3_ref[R:].astype(F32))).astype(BF)


def solve_last_body(side_ref, diag_ref, g_ref, a_ref, r_ref, t01_ref, t23_ref, t_ref):
    last = LEVELS - 1
    t = solve(
        diag_ref[last, 0],
        diag_ref[last, 1],
        side_ref[last] == 1,
        a_ref[...].astype(F32),
        r_ref[...].astype(F32),
        g_ref[last],
    )
    t_ref[: 2 * R] = t01_ref[...]
    t_ref[2 * R : 4 * R] = t23_ref[...]
    t_ref[4 * R :] = t.astype(BF)


def columns_body(y_ref, *refs):
    ins, out_ref = refs[:-1], refs[-1]
    for d in range(Y):
        at = pl.ds(pl.multiple_of(((y_ref[0] + d) & (Y - 1)) * R, R), R)
        row = 0
        for ref in ins[d::Y]:
            out_ref[row : row + ref.shape[0], at] = ref[...]
            row += ref.shape[0]


def gather_y(block):
    return [block, to_y(block, -1), to_y(block, 2), to_y(block, 1)]


def gather_columns(y, *ts):
    blocks = [b for t in ts for b in gather_y(t)]
    rows = sum(t.shape[0] for t in ts)
    return kernel_call(
        columns_body, jax.ShapeDtypeStruct((rows, Y * R), BF), 1, len(blocks), name="columns"
    )(y[None], *blocks)


def update_body(c_ref, y_own_ref, y_oth_ref, u_ref, t_own_ref, t_oth_ref, out_ref, held, sems):
    rows, half = y_own_ref.shape
    tiles = sems.shape[0]
    tile = rows // tiles
    c = c_ref[0]
    copies = []
    for i in range(tiles):
        at_row = pl.ds(i * tile, tile)
        for y_ref, t_ref, core in ((y_own_ref, t_own_ref, c), (y_oth_ref, t_oth_ref, 1 - c)):
            at = pl.ds(pl.multiple_of(core * half, half), half)
            held[at_row, at] = y_ref[at_row, :] - dot(u_ref[at_row, :], t_ref[...])
        copy = pltpu.make_async_copy(held.at[at_row], out_ref.at[at_row], sems.at[i])
        copy.start()
        copies.append(copy)
    for copy in copies:
        copy.wait()


def update(c, y_own, y_oth, u, t_own, t_oth):
    rows, half = y_own.shape
    vmem = pl.BlockSpec(memory_space=pltpu.VMEM)
    return pl.pallas_call(
        update_body,
        out_shape=jax.ShapeDtypeStruct((rows, 2 * half), F32),
        in_specs=[pl.BlockSpec(memory_space=pltpu.SMEM)] + [vmem] * 5,
        out_specs=pl.BlockSpec(memory_space=pl.ANY),
        scratch_shapes=[pltpu.VMEM((rows, 2 * half), F32), pltpu.SemaphoreType.DMA((4,))],
        compiler_params=pltpu.CompilerParams(vmem_limit_bytes=VMEM_LIMIT),
        name="update",
    )(c[None], y_own, y_oth, u, t_own, t_oth)


def shards(rhs, leaf_inverse, leaf_sizes, u_tilde, v_right, cap_factor):
    rows, columns = rhs.shape
    row = lax.axis_index("row").astype(jnp.int32)
    partner = lax.axis_index("partner").astype(jnp.int32)
    y, c = row >> 1, row & 1
    side = (partner >> jnp.arange(LEVELS, dtype=jnp.int32)) & 1
    scalars = jnp.stack([row * rows, c, leaf_sizes[0], y])
    g = cap_factor[:, 0]
    struct = jax.ShapeDtypeStruct

    a_oth = to_core(leaf_inverse)
    part_shape = struct((rows, columns // C), BF)
    mine, theirs = kernel_call(live_rhs_body, (part_shape, part_shape), 1, 1, name="live_rhs")(
        scalars, rhs
    )
    other = to_core(theirs)

    half, part = R // 2, R // C // Y
    half_struct = struct((N_CAP, half, R), F32)
    u_rows, vt, cap_mine, cap_theirs = kernel_call(
        prepare_body,
        (
            struct((rows, LEVELS * R), BF),
            struct((LEVELS * R, rows), BF),
            half_struct,
            half_struct,
        ),
        1,
        2,
        scratch=[pltpu.VMEM((N_CAP, R, R), F32)],
        name="prepare",
    )(scalars, u_tilde, v_right)
    part_struct = struct((N_CAP, part, R), BF)
    own, s1, s2, s3 = kernel_call(
        cap_parts_body,
        (struct((N_CAP, part, R), F32), part_struct, part_struct, part_struct),
        1,
        2,
        name="cap_parts",
    )(scalars, cap_mine, to_core(cap_theirs))
    part1, part2, part3 = to_y(s1, 1), to_y(s2, 2), to_y(s3, 3)

    vt_oth = to_core(vt)
    chip = kernel_call(
        chip_body, struct((C * rows, columns // C), BF), 1, 2, name="chip"
    )(scalars, after(mine, part1, part2, part3, a_oth, vt_oth), other)
    before, behind = to_y(chip, 1), to_y(chip, -1)
    cap_leaf = kernel_call(cap_leaf_body, struct((N_CAP, part, R), F32), 0, 4, name="cap_leaf")(
        own, part1, part2, part3
    )
    low, cap_quad = kernel_call(
        cap_x_body,
        (struct((2, FIRST[2], part, R), BF), struct((N_CAP - FIRST[2], part, R), F32)),
        0,
        4,
        name="cap_x",
    )(cap_leaf, to_x(cap_leaf, 1), to_x(cap_leaf, 2), to_x(cap_leaf, 3))
    mid, last = kernel_call(
        cap_z_body,
        (struct((2, FIRST[4] - FIRST[2], part, R), BF), struct((1, part, R), F32)),
        0,
        4,
        name="cap_z",
    )(cap_quad, to_z(cap_quad, 1), to_z(cap_quad, 2), to_z(cap_quad, 3))
    both = kernel_call(
        cap_both_body, struct((2 * N_CAP, part, R), BF), 0, 4, name="cap_both"
    )(low, mid, last, to_z(last, 4))
    top, bottom = kernel_call(
        halves_body, (part_shape, part_shape), 0, 2, name="halves"
    )(after(before, both), behind)
    far_top, far_bottom = to_y(top, 1), to_y(bottom, -1)
    places = jnp.stack([y, c, leaf_sizes[0]])
    along = [(y + d) & (Y - 1) for d in range(Y)]
    sums = leaf(
        places, [along[0], along[3], along[1]], leaf_inverse, a_oth, [chip, before, behind]
    )
    both = after(both, top)
    cap_rows = kernel_call(
        cap_stack_body, struct((2 * N_CAP, half, R), BF), 1, 4, name="cap_stack"
    )(scalars, *gather_y(both))
    h, diag = kernel_call(
        elimination_body,
        (struct((N_H * R, 2 * R), BF), struct((LEVELS, 2, R, R), BF)),
        2,
        3,
        scratch=[pltpu.VMEM((2 * N_CAP, R, R), BF)],
        name="elimination",
    )(scalars, side, cap_rows, to_core(cap_rows), g)

    places = after(places, cap_rows)
    y_own, y_oth, *q = leaf(
        places, [along[2]], leaf_inverse, a_oth, [far_top, far_bottom], [*sums, vt, vt_oth]
    )
    y_other = to_core(y_oth)

    e, e_up = kernel_call(
        eliminate_body,
        (struct((LEVELS * R, R), BF), struct(((LEVELS - 1) * R, R), BF)),
        0,
        5,
        name="eliminate",
    )(q[0], to_y(q[1], 1), to_y(q[2], 2), to_y(q[3], 3), after(h, y_other))
    two = struct((2 * R, R), BF)
    r1, r2, r3 = to_x(e, 1), to_x(e_up, 2), to_x(e_up, 3)
    quad, quad_up = kernel_call(
        quad_body, (struct((3 * R, R), BF), struct((2 * R, R), BF)), 0, 4, name="quad"
    )(e, r1, r2, r3)
    z1, z2, z3 = to_z(quad, 1), to_z(quad_up, 2), to_z(quad_up, 3)
    t01 = kernel_call(
        lambda *refs: solve_two_body((0, 1), *refs), two, 1, 6, name="solve_0_1"
    )(side, diag, g, after(e, quad), r1, r2, r3)
    own4 = kernel_call(own4_body, struct((R, R), BF), 0, 4, name="own4")(quad, z1, z2, z3)
    sib4 = to_z(own4, 4)
    t23 = kernel_call(
        lambda *refs: solve_two_body((2, 3), *refs), two, 1, 6, name="solve_2_3"
    )(side, diag, g, after(quad, own4), z1, z2, z3)
    t = kernel_call(solve_last_body, struct((LEVELS * R, R), BF), 1, 6, name="solve_4")(
        side, diag, g, own4, sib4, t01, t23
    )
    t_own = gather_columns(y, t)
    t_oth = to_core(t_own)
    return update(c, y_own, y_other, u_rows, t_own, t_oth)


def solution(mesh):
    return jax.shard_map(
        shards,
        mesh=mesh,
        in_specs=(
            P(("partner", "row"), None),
            P(("partner", "row"), None),
            P("partner"),
            P(None, ("partner", "row"), None),
            P(None, ("partner", "row"), None),
            P(None, "partner", None, None),
        ),
        out_specs=P(("partner", "row"), None),
        check_vma=False,
    )
```

```python
import jax
import jax.numpy as jnp
from jax import lax
from jax.experimental import pallas as pl
from jax.experimental.pallas import tpu as pltpu
from jax.sharding import PartitionSpec as P

Z, X, Y, C = 8, 4, 4, 2
LEVELS = 5
R = 128
BF = jnp.bfloat16
F32 = jnp.float32
FIRST = (0, 5, 9, 12, 14)
N_CAP = 15
H_FIRST = (0, 4, 7, 9)
N_H = 10
VMEM_LIMIT = 16 * 1024 * 1024


def move(block, where):
    route = []
    for z in range(Z):
        for x in range(X):
            for y in range(Y):
                for c in range(C):
                    z1, x1, y1, c1 = where(z, x, y, c)
                    here = ((z * X + x) * Y + y) * C + c
                    there = ((z1 % Z * X + x1 % X) * Y + y1 % Y) * C + c1 % C
                    route.append((here, there))
    return lax.ppermute(block, ("partner", "row"), route)


def after(block, *others):
    return lax.optimization_barrier((block, *others))[0]


def in_hbm(block):
    return pltpu.with_memory_space_constraint(block, pltpu.HBM)


def to_core(block):
    return move(block, lambda z, x, y, c: (z, x, y, 1 - c))


def to_y(block, d):
    return move(block, lambda z, x, y, c: (z, x, y + d, c))


def to_x(block, mask):
    return move(block, lambda z, x, y, c: (z, x ^ mask, y, c))


def to_z(block, mask):
    return move(block, lambda z, x, y, c: (z ^ mask, x, y, c))


def dot(a, b):
    return jnp.dot(a, b, preferred_element_type=F32)


def split(a):
    upper = a.astype(BF)
    return upper, (a - upper.astype(F32)).astype(BF)


def dot_16_32(a, b):
    upper, lower = split(b)
    return dot(a, upper) + dot(a, lower)


def dot_32_32(a, b):
    a_upper, a_lower = split(a)
    b_upper, b_lower = split(b)
    return dot(a_upper, b_upper) + (dot(a_upper, b_lower) + dot(a_lower, b_upper))


def kernel_call(body, out_shape, n_scalar, n_in, scratch=(), name=None):
    smem = pl.BlockSpec(memory_space=pltpu.SMEM)
    vmem = pl.BlockSpec(memory_space=pltpu.VMEM)
    outs = out_shape if isinstance(out_shape, (tuple, list)) else (out_shape,)
    out_specs = [vmem] * len(outs)
    return pl.pallas_call(
        body,
        out_shape=out_shape,
        in_specs=[smem] * n_scalar + [vmem] * n_in,
        out_specs=out_specs if isinstance(out_shape, (tuple, list)) else vmem,
        scratch_shapes=list(scratch),
        compiler_params=pltpu.CompilerParams(vmem_limit_bytes=VMEM_LIMIT),
        name=name,
    )


def side_bits(upper, own, sib):
    return jnp.where(upper, sib, own), jnp.where(upper, own, sib)


def live_rhs_body(scalar_ref, rhs_hbm, mine_ref, theirs_ref, rhs_ref, sems):
    first, c = scalar_ref[0], scalar_ref[1]
    rows, half = mine_ref.shape
    tiles = sems.shape[0]
    tile = rows // tiles
    spans = [pl.ds(i * tile, tile) for i in range(tiles)]
    loads = [
        pltpu.make_async_copy(rhs_hbm.at[at], rhs_ref.at[at], sems.at[i])
        for i, at in enumerate(spans)
    ]
    for load in loads:
        load.start()
    iota = lax.broadcasted_iota(jnp.int32, (tile, 1), 0)
    for i, (load, at) in enumerate(zip(loads, spans)):
        load.wait()
        live = first + i * tile + iota < scalar_ref[2]
        for ref, core in ((mine_ref, c), (theirs_ref, 1 - c)):
            part = rhs_ref[at, pl.ds(pl.multiple_of(core * half, half), half)]
            ref[at, :] = jnp.where(live, part, 0.0).astype(BF)


def live_rhs(scalars, rhs):
    rows, columns = rhs.shape
    vmem = pl.BlockSpec(memory_space=pltpu.VMEM)
    out = jax.ShapeDtypeStruct((rows, columns // C), BF)
    return pl.pallas_call(
        live_rhs_body,
        out_shape=(out, out),
        in_specs=[pl.BlockSpec(memory_space=pltpu.SMEM), pl.BlockSpec(memory_space=pltpu.HBM)],
        out_specs=(vmem, vmem),
        scratch_shapes=[pltpu.VMEM(rhs.shape, F32), pltpu.SemaphoreType.DMA((4,))],
        compiler_params=pltpu.CompilerParams(vmem_limit_bytes=VMEM_LIMIT),
        name="live_rhs",
    )(scalars, rhs)


def chip_body(scalar_ref, mine_ref, other_ref, chip_ref):
    c = scalar_ref[1]
    rows = mine_ref.shape[0]
    for ref, core in ((mine_ref, c), (other_ref, 1 - c)):
        chip_ref[pl.ds(pl.multiple_of(core * rows, rows), rows), :] = ref[...]


def halves_body(before_ref, behind_ref, top_ref, bottom_ref):
    rows = top_ref.shape[0]
    top_ref[...] = before_ref[:rows]
    bottom_ref[...] = behind_ref[rows:]


def prepare_body(
    scalar_ref,
    u_hbm,
    v_hbm,
    vt_ref,
    mine_ref,
    theirs_ref,
    u_ref,
    v_ref,
    rows_ref,
    cap_ref,
    sems,
):
    loads = [
        pltpu.make_async_copy(u_hbm, u_ref, sems.at[0]),
        pltpu.make_async_copy(v_hbm, v_ref, sems.at[1]),
    ]
    for load in loads:
        load.start()
    rows = u_ref.shape[1]
    first, c = scalar_ref[0], scalar_ref[1]
    live = first + lax.broadcasted_iota(jnp.int32, (rows, 1), 0) < scalar_ref[2]
    loads[0].wait()
    for l in range(LEVELS):
        rows_ref[:, l * R : (l + 1) * R] = jnp.where(live, u_ref[l].astype(F32), 0.0).astype(BF)
    loads[1].wait()
    for l in range(LEVELS):
        vt_ref[l * R : (l + 1) * R, :] = v_ref[l].T
    for l in range(LEVELS):
        cap = dot(vt_ref[l * R : (l + 1) * R, :], rows_ref[:, : (l + 1) * R])
        for m in range(l + 1):
            cap_ref[FIRST[m] + l - m] = cap[:, m * R : (m + 1) * R]
    half = R // 2
    mine_ref[...] = cap_ref[:, pl.ds(pl.multiple_of(c * half, half), half), :]
    theirs_ref[...] = cap_ref[:, pl.ds(pl.multiple_of((1 - c) * half, half), half), :]


def prepare(scalars, u, v):
    levels, rows, _ = u.shape
    half = jax.ShapeDtypeStruct((N_CAP, R // 2, R), F32)
    hbm = pl.BlockSpec(memory_space=pltpu.HBM)
    vmem = pl.BlockSpec(memory_space=pltpu.VMEM)
    return pl.pallas_call(
        prepare_body,
        out_shape=(
            jax.ShapeDtypeStruct((levels * R, rows), BF),
            half,
            half,
        ),
        in_specs=[pl.BlockSpec(memory_space=pltpu.SMEM), hbm, hbm],
        out_specs=(vmem, vmem, vmem),
        scratch_shapes=[
            pltpu.VMEM(u.shape, BF),
            pltpu.VMEM(v.shape, BF),
            pltpu.VMEM((rows, levels * R), BF),
            pltpu.VMEM((N_CAP, R, R), F32),
            pltpu.SemaphoreType.DMA((2,)),
        ],
        compiler_params=pltpu.CompilerParams(vmem_limit_bytes=VMEM_LIMIT),
        name="prepare",
    )(scalars, u, v)


def cap_parts_body(scalar_ref, mine_ref, other_ref, own_ref, *send_refs):
    y = scalar_ref[3]
    part = own_ref.shape[1]

    def at(d):
        return pl.ds(pl.multiple_of(((y + d) & (Y - 1)) * part, part), part)

    own_ref[...] = mine_ref[:, at(0), :] + other_ref[:, at(0), :]
    for d, ref in enumerate(send_refs):
        ref[...] = (mine_ref[:, at(d + 1), :] + other_ref[:, at(d + 1), :]).astype(BF)


def cap_leaf_body(own_ref, r1_ref, r2_ref, r3_ref, leaf_ref):
    leaf_ref[...] = (own_ref[...] + r1_ref[...].astype(F32)) + (
        r2_ref[...].astype(F32) + r3_ref[...].astype(F32)
    )


def cap_x_body(leaf_ref, r1_ref, r2_ref, r3_ref, low_ref, quad_ref):
    n0, n1 = FIRST[1], FIRST[2]
    low_ref[0, :n0] = leaf_ref[:n0].astype(BF)
    low_ref[1, :n0] = r1_ref[:n0].astype(BF)
    low_ref[0, n0:] = (leaf_ref[n0:n1] + r1_ref[n0:n1]).astype(BF)
    low_ref[1, n0:] = (r2_ref[n0:n1] + r3_ref[n0:n1]).astype(BF)
    quad_ref[...] = (leaf_ref[n1:] + r1_ref[n1:]) + (r2_ref[n1:] + r3_ref[n1:])


def cap_z_body(quad_ref, z1_ref, z2_ref, z3_ref, mid_ref, last_ref):
    n0, n1 = FIRST[3] - FIRST[2], FIRST[4] - FIRST[2]
    mid_ref[0, :n0] = quad_ref[:n0].astype(BF)
    mid_ref[1, :n0] = z1_ref[:n0].astype(BF)
    mid_ref[0, n0:] = (quad_ref[n0:n1] + z1_ref[n0:n1]).astype(BF)
    mid_ref[1, n0:] = (z2_ref[n0:n1] + z3_ref[n0:n1]).astype(BF)
    last_ref[...] = (quad_ref[n1:] + z1_ref[n1:]) + (z2_ref[n1:] + z3_ref[n1:])


def cap_both_body(low_ref, mid_ref, own4_ref, sib4_ref, both_ref):
    for side, last_ref in enumerate((own4_ref, sib4_ref)):
        at = side * N_CAP
        both_ref[at : at + FIRST[2]] = low_ref[side]
        both_ref[at + FIRST[2] : at + FIRST[4]] = mid_ref[side]
        both_ref[at + FIRST[4]] = last_ref[0].astype(BF)


def cap_stack_body(scalar_ref, b0_ref, b1_ref, b2_ref, b3_ref, out_ref):
    part = b0_ref.shape[1]
    for d, ref in enumerate((b0_ref, b1_ref, b2_ref, b3_ref)):
        at = ((scalar_ref[3] + d) & (Y - 1)) * part
        out_ref[:, pl.ds(pl.multiple_of(at, part), part), :] = ref[...]


def elimination_body(scalar_ref, side_ref, mine_ref, other_ref, g_ref, h_ref, diag_ref, all_ref):
    c = scalar_ref[1]
    half = R // 2
    all_ref[:, pl.ds(pl.multiple_of(c * half, half), half), :] = mine_ref[...]
    all_ref[:, pl.ds(pl.multiple_of((1 - c) * half, half), half), :] = other_ref[...]
    rows = lax.broadcasted_iota(jnp.int32, (R, R), 0)
    cols = lax.broadcasted_iota(jnp.int32, (R, R), 1)
    eye = (rows == cols).astype(F32)
    for m in range(LEVELS):
        upper = side_ref[m] == 1
        first = FIRST[m]
        c0, c1 = side_bits(upper, all_ref[first], all_ref[N_CAP + first])
        diag_ref[m, 0] = c0
        diag_ref[m, 1] = c1
        if m == LEVELS - 1:
            break
        g = g_ref[m]
        g_hi, g_lo = split(g)
        gc0 = dot(g_hi, c0) + dot(g_lo, c0)
        m1 = jnp.where(upper, -gc0, g)
        m0 = jnp.where(upper, eye, 0.0) - dot_16_32(c1, m1)
        m0_hi, m0_lo = split(m0)
        m1_hi, m1_lo = split(m1)
        for l in range(m + 1, LEVELS):
            j = first + l - m
            a0, a1 = side_bits(upper, all_ref[j], all_ref[N_CAP + j])
            h = dot(a0, m0_hi) + dot(a0, m0_lo) + dot(a1, m1_hi) + dot(a1, m1_lo)
            hi, lo = split(h)
            at = (H_FIRST[m] + l - m - 1) * R
            h_ref[at : at + R, 0:R] = hi
            h_ref[at : at + R, R : 2 * R] = lo


def leaf_body(
    chip_ref, a0_hbm, a1_hbm, b0_ref, b1_ref, b2_ref, sum0, sum1, far0, far1, buffers, sems
):
    depth = b0_ref.shape[0]
    loads = []
    for k in range(Y):
        at = pl.ds(pl.multiple_of(chip_ref[k] * depth, depth), depth)
        for i, (a_hbm, far) in enumerate(((a0_hbm, far0), (a1_hbm, far1))):
            to = far if k == Y - 1 else buffers.at[k, i]
            loads.append(pltpu.make_async_copy(a_hbm.at[:, at], to, sems.at[k, i]))
    for load in loads:
        load.start()
    for k, block in enumerate((b0_ref, b1_ref, b2_ref)):
        for i, total in enumerate((sum0, sum1)):
            loads[2 * k + i].wait()
            new = dot(buffers[k, i], block[...])
            total[...] = new if k == 0 else total[...] + new
    for load in loads[2 * (Y - 1) :]:
        load.wait()


def leaf(chips, a_own, a_oth, blocks):
    rows = a_own.shape[0]
    depth, half = blocks[0].shape
    vmem = pl.BlockSpec(memory_space=pltpu.VMEM)
    hbm = pl.BlockSpec(memory_space=pltpu.HBM)
    out_shape = [jax.ShapeDtypeStruct((rows, half), F32)] * 2
    out_shape += [jax.ShapeDtypeStruct((rows, depth), BF)] * 2
    return pl.pallas_call(
        leaf_body,
        out_shape=out_shape,
        in_specs=[pl.BlockSpec(memory_space=pltpu.SMEM), hbm, hbm] + [vmem] * 3,
        out_specs=[vmem] * 4,
        scratch_shapes=[
            pltpu.VMEM((Y - 1, 2, rows, depth), BF),
            pltpu.SemaphoreType.DMA((Y, 2)),
        ],
        compiler_params=pltpu.CompilerParams(vmem_limit_bytes=VMEM_LIMIT),
        name="leaf",
    )(jnp.stack(chips), a_own, a_oth, *blocks)


def project(block, y_refs, v_refs):
    at = pl.ds(pl.multiple_of((block & (Y - 1)) * R, R), R)
    q = None
    for y_ref, v_ref in zip(y_refs, v_refs):
        hi, lo = split(y_ref[:, at])
        new = dot(v_ref[...], jnp.concatenate([hi, lo], axis=1))
        q = new if q is None else q + new
    return (q[:, :R] + q[:, R:]).astype(BF)


def leaf_end_body(
    scalar_ref, a0_ref, a1_ref, top_ref, bottom_ref, sum0_ref, sum1_ref, va_ref, vb_ref, *out_refs
):
    y_refs, q_refs = out_refs[:2], out_refs[2:]
    rows = y_refs[0].shape[0]
    y, c, size = scalar_ref[0], scalar_ref[1], scalar_ref[2]
    iota = lax.broadcasted_iota(jnp.int32, (rows, 1), 0)
    far = jnp.concatenate([top_ref[...], bottom_ref[...]], axis=0)
    for a_ref, sum_ref, y_ref, core in zip(
        (a0_ref, a1_ref), (sum0_ref, sum1_ref), y_refs, (c, 1 - c)
    ):
        new = dot(a_ref[...], far)
        live = (y * C + core) * rows + iota < size
        y_ref[...] = jnp.where(live, sum_ref[...] + new, 0.0)
    for d, q_ref in enumerate(q_refs):
        q_ref[...] = project(y + d + 1, y_refs, (va_ref, vb_ref))


def project_own_body(place_ref, y0_ref, y1_ref, va_ref, vb_ref, q_ref):
    q_ref[...] = project(place_ref[0], (y0_ref, y1_ref), (va_ref, vb_ref))


def eliminate_body(q0_ref, q1_ref, q2_ref, q3_ref, h_ref, e_ref, upper_ref):
    q = (q0_ref[...].astype(F32) + q1_ref[...].astype(F32)) + (
        q2_ref[...].astype(F32) + q3_ref[...].astype(F32)
    )
    for m in range(LEVELS):
        e = q[:R].astype(BF)
        e_ref[m * R : (m + 1) * R, :] = e
        if m > 0:
            upper_ref[(m - 1) * R : m * R, :] = e
        if m < LEVELS - 1:
            at, n = H_FIRST[m] * R, (LEVELS - 1 - m) * R
            q = q[R:] - dot(h_ref[at : at + n, :], jnp.concatenate([e, e], axis=0))


def solve(c0, c1, upper, own, sib, g):
    s0, s1 = side_bits(upper, own, sib)
    inner = s0 - dot_16_32(c0, s1)
    t1 = dot_32_32(g, inner)
    t0 = s1 - dot_16_32(c1, t1)
    return jnp.where(upper, t1, t0)


def solve_two_body(levels, side_ref, diag_ref, g_ref, a_ref, r1_ref, r2_ref, r3_ref, t_ref):
    low, high = levels
    one = slice(0, R)
    two = slice(R, 2 * R)
    t = solve(
        diag_ref[low, 0],
        diag_ref[low, 1],
        side_ref[low] == 1,
        a_ref[one].astype(F32),
        r1_ref[one].astype(F32),
        g_ref[low],
    )
    t_ref[one] = t.astype(BF)
    t = solve(
        diag_ref[high, 0],
        diag_ref[high, 1],
        side_ref[high] == 1,
        a_ref[two].astype(F32) + r1_ref[two].astype(F32),
        r2_ref[one].astype(F32) + r3_ref[one].astype(F32),
        g_ref[high],
    )
    t_ref[two] = t.astype(BF)


def quad_body(e_ref, r1_ref, r2_ref, r3_ref, quad_ref, upper_ref):
    two = slice(2 * R, 5 * R)
    quad = e_ref[two].astype(F32) + r1_ref[two].astype(F32)
    quad = quad + (r2_ref[R:].astype(F32) + r3_ref[R:].astype(F32))
    quad = quad.astype(BF)
    quad_ref[...] = quad
    upper_ref[...] = quad[R:]


def own4_body(quad_ref, z1_ref, z2_ref, z3_ref, own_ref):
    own = quad_ref[2 * R :].astype(F32) + z1_ref[2 * R :].astype(F32)
    own_ref[...] = (own + (z2_ref[R:].astype(F32) + z3_ref[R:].astype(F32))).astype(BF)


def solve_last_body(side_ref, diag_ref, g_ref, a_ref, r_ref, t01_ref, t23_ref, t_ref):
    last = LEVELS - 1
    t = solve(
        diag_ref[last, 0],
        diag_ref[last, 1],
        side_ref[last] == 1,
        a_ref[...].astype(F32),
        r_ref[...].astype(F32),
        g_ref[last],
    )
    t_ref[: 2 * R] = t01_ref[...]
    t_ref[2 * R : 4 * R] = t23_ref[...]
    t_ref[4 * R :] = t.astype(BF)


def columns_body(y_ref, b0_ref, b1_ref, b2_ref, b3_ref, out_ref):
    for d, ref in enumerate((b0_ref, b1_ref, b2_ref, b3_ref)):
        at = ((y_ref[0] + d) & (Y - 1)) * R
        out_ref[:, pl.ds(pl.multiple_of(at, R), R)] = ref[...]


def gather_y(block):
    return [block, to_y(block, -1), to_y(block, 2), to_y(block, 1)]


def put_columns(y, blocks):
    out = jax.ShapeDtypeStruct((blocks[0].shape[0], Y * R), BF)
    return kernel_call(columns_body, out, 1, Y, name="columns")(y[None], *blocks)


def bring_body(*refs):
    n = (len(refs) - 1) // 2
    sems = refs[-1]
    copies = [
        pltpu.make_async_copy(refs[i], refs[n + i], sems.at[i]) for i in range(n)
    ]
    for copy in copies:
        copy.start()
    for copy in copies:
        copy.wait()


def bring(*arrays):
    n = len(arrays)
    size = sum(a.size * a.dtype.itemsize for a in arrays)
    return pl.pallas_call(
        bring_body,
        out_shape=[jax.ShapeDtypeStruct(a.shape, a.dtype) for a in arrays],
        in_specs=[pl.BlockSpec(memory_space=pltpu.HBM)] * n,
        out_specs=[pl.BlockSpec(memory_space=pltpu.VMEM)] * n,
        scratch_shapes=[pltpu.SemaphoreType.DMA((n,))],
        compiler_params=pltpu.CompilerParams(vmem_limit_bytes=VMEM_LIMIT),
        cost_estimate=pl.CostEstimate(flops=0, bytes_accessed=2 * size, transcendentals=0),
        name="bring",
    )(*[in_hbm(a) for a in arrays])


def update_body(scalar_ref, y0_ref, y1_ref, u_ref, t0_ref, t1_ref, out_hbm, held, sems):
    rows, half = y0_ref.shape
    tiles = sems.shape[0]
    tile = rows // tiles
    first, c, size = scalar_ref[0], scalar_ref[1], scalar_ref[2]
    iota = lax.broadcasted_iota(jnp.int32, (tile, 1), 0)
    copies = []
    for i in range(tiles):
        at_row = pl.ds(i * tile, tile)
        u = jnp.concatenate([u_ref[l, at_row, :] for l in range(LEVELS)], axis=1)
        live = first + i * tile + iota < size
        for y_ref, t_ref, core in ((y0_ref, t0_ref, c), (y1_ref, t1_ref, 1 - c)):
            at = pl.ds(pl.multiple_of(core * half, half), half)
            held[at_row, at] = y_ref[at_row, :] - jnp.where(live, dot(u, t_ref[...]), 0.0)
        copy = pltpu.make_async_copy(held.at[at_row], out_hbm.at[at_row], sems.at[i])
        copy.start()
        copies.append(copy)
    for copy in copies:
        copy.wait()


def update(scalars, y_own, y_oth, u, t_own, t_oth):
    rows, half = y_own.shape
    vmem = pl.BlockSpec(memory_space=pltpu.VMEM)
    return pl.pallas_call(
        update_body,
        out_shape=jax.ShapeDtypeStruct((rows, 2 * half), F32),
        in_specs=[pl.BlockSpec(memory_space=pltpu.SMEM)] + [vmem] * 5,
        out_specs=pl.BlockSpec(memory_space=pl.ANY),
        scratch_shapes=[pltpu.VMEM((rows, 2 * half), F32), pltpu.SemaphoreType.DMA((4,))],
        compiler_params=pltpu.CompilerParams(vmem_limit_bytes=VMEM_LIMIT),
        name="update",
    )(scalars, y_own, y_oth, u, t_own, t_oth)


def shards(rhs, leaf_inverse, leaf_sizes, u_tilde, v_right, cap_factor):
    rows, columns = rhs.shape
    row = lax.axis_index("row").astype(jnp.int32)
    partner = lax.axis_index("partner").astype(jnp.int32)
    y, c = row >> 1, row & 1
    side = (partner >> jnp.arange(LEVELS, dtype=jnp.int32)) & 1
    scalars = jnp.stack([row * rows, c, leaf_sizes[0], y])
    g = cap_factor[:, 0]
    struct = jax.ShapeDtypeStruct

    a_oth = to_core(leaf_inverse)
    part_shape = struct((rows, columns // C), BF)
    mine, theirs = live_rhs(scalars, in_hbm(rhs))
    other = to_core(theirs)

    half, part = R // 2, R // C // Y
    vt, cap_mine, cap_theirs = prepare(scalars, in_hbm(u_tilde), in_hbm(v_right))
    part_struct = struct((N_CAP, part, R), BF)
    own, s1, s2, s3 = kernel_call(
        cap_parts_body,
        (struct((N_CAP, part, R), F32), part_struct, part_struct, part_struct),
        1,
        2,
        name="cap_parts",
    )(scalars, cap_mine, to_core(cap_theirs))
    part1, part2, part3 = to_y(s1, 1), to_y(s2, 2), to_y(s3, 3)

    vt_oth = to_core(vt)
    chip = kernel_call(
        chip_body, struct((C * rows, columns // C), BF), 1, 2, name="chip"
    )(scalars, after(mine, part1, a_oth, vt_oth), other)
    before, behind = to_y(chip, 1), to_y(after(chip, part2, part3), -1)
    cap_leaf = kernel_call(cap_leaf_body, struct((N_CAP, part, R), F32), 0, 4, name="cap_leaf")(
        own, part1, part2, part3
    )
    low, cap_quad = kernel_call(
        cap_x_body,
        (struct((2, FIRST[2], part, R), BF), struct((N_CAP - FIRST[2], part, R), F32)),
        0,
        4,
        name="cap_x",
    )(cap_leaf, to_x(cap_leaf, 1), to_x(cap_leaf, 2), to_x(cap_leaf, 3))
    mid, last = kernel_call(
        cap_z_body,
        (struct((2, FIRST[4] - FIRST[2], part, R), BF), struct((1, part, R), F32)),
        0,
        4,
        name="cap_z",
    )(cap_quad, to_z(cap_quad, 1), to_z(cap_quad, 2), to_z(cap_quad, 3))
    both = kernel_call(
        cap_both_body, struct((2 * N_CAP, part, R), BF), 0, 4, name="cap_both"
    )(low, mid, last, to_z(last, 4))
    top, bottom = kernel_call(
        halves_body, (part_shape, part_shape), 0, 2, name="halves"
    )(after(before, both), behind)
    far_top, far_bottom = to_y(top, 1), to_y(bottom, -1)
    places = jnp.stack([y, c, leaf_sizes[0]])
    along = [(y + d) & (Y - 1) for d in range(Y)]
    sum_own, sum_oth, far_own, far_oth = leaf(
        [along[0], along[3], along[1], along[2]],
        in_hbm(leaf_inverse),
        in_hbm(a_oth),
        [chip, before, behind],
    )
    both = after(both, top)
    cap_rows = kernel_call(
        cap_stack_body, struct((2 * N_CAP, half, R), BF), 1, 4, name="cap_stack"
    )(scalars, *gather_y(both))
    h, diag = kernel_call(
        elimination_body,
        (struct((N_H * R, 2 * R), BF), struct((LEVELS, 2, R, R), BF)),
        2,
        3,
        scratch=[pltpu.VMEM((2 * N_CAP, R, R), BF)],
        name="elimination",
    )(scalars, side, cap_rows, to_core(cap_rows), g)

    places = after(places, cap_rows)
    y_own, y_oth, *q = kernel_call(
        leaf_end_body,
        [struct((rows, columns // C), F32)] * 2 + [struct((LEVELS * R, R), BF)] * (Y - 1),
        1,
        8,
        name="leaf_end",
    )(places, far_own, far_oth, far_top, far_bottom, sum_own, sum_oth, vt, vt_oth)
    q_own = kernel_call(
        project_own_body, struct((LEVELS * R, R), BF), 1, 4, name="project_own"
    )(places, y_own, y_oth, vt, vt_oth)
    y_other = to_core(y_oth)

    e, e_up = kernel_call(
        eliminate_body,
        (struct((LEVELS * R, R), BF), struct(((LEVELS - 1) * R, R), BF)),
        0,
        5,
        name="eliminate",
    )(q_own, to_y(q[0], 1), to_y(q[1], 2), to_y(q[2], 3), after(h, y_other))
    two = struct((2 * R, R), BF)
    r1, r2, r3 = to_x(e, 1), to_x(e_up, 2), to_x(e_up, 3)
    quad, quad_up = kernel_call(
        quad_body, (struct((3 * R, R), BF), struct((2 * R, R), BF)), 0, 4, name="quad"
    )(e, r1, r2, r3)
    z1, z2, z3 = to_z(quad, 1), to_z(quad_up, 2), to_z(quad_up, 3)
    t01 = kernel_call(
        lambda *refs: solve_two_body((0, 1), *refs), two, 1, 6, name="solve_0_1"
    )(side, diag, g, after(e, quad), r1, r2, r3)
    own4 = kernel_call(own4_body, struct((R, R), BF), 0, 4, name="own4")(
        after(quad, t01), z1, z2, z3
    )
    sib4 = to_z(own4, 4)
    t23 = kernel_call(
        lambda *refs: solve_two_body((2, 3), *refs), two, 1, 6, name="solve_2_3"
    )(side, diag, g, after(quad, own4), z1, z2, z3)
    t = kernel_call(solve_last_body, struct((LEVELS * R, R), BF), 1, 6, name="solve_4")(
        side, diag, g, own4, sib4, t01, t23
    )
    t_own = put_columns(y, gather_y(t))
    t_oth = to_core(t_own)
    return update(scalars, *bring(y_own, y_other, u_tilde), t_own, t_oth)


def solution(mesh):
    return jax.shard_map(
        shards,
        mesh=mesh,
        in_specs=(
            P(("partner", "row"), None),
            P(("partner", "row"), None),
            P("partner"),
            P(None, ("partner", "row"), None),
            P(None, ("partner", "row"), None),
            P(None, "partner", None, None),
        ),
        out_specs=P(("partner", "row"), None),
        check_vma=False,
    )
```

```python
import jax
import jax.numpy as jnp
from jax import lax
from jax.experimental import pallas as pl
from jax.experimental.pallas import tpu as pltpu
from jax.sharding import PartitionSpec as P

Z, X, Y, C = 8, 4, 4, 2
LEVELS = 5
R = 128
BF = jnp.bfloat16
F32 = jnp.float32
FIRST = (0, 5, 9, 12, 14)
N_CAP = 15
H_FIRST = (0, 4, 7, 9)
N_H = 10
VMEM_LIMIT = 16 * 1024 * 1024


def move(block, where):
    route = []
    for z in range(Z):
        for x in range(X):
            for y in range(Y):
                for c in range(C):
                    z1, x1, y1, c1 = where(z, x, y, c)
                    here = ((z * X + x) * Y + y) * C + c
                    there = ((z1 % Z * X + x1 % X) * Y + y1 % Y) * C + c1 % C
                    route.append((here, there))
    return lax.ppermute(block, ("partner", "row"), route)


def after(block, *others):
    return lax.optimization_barrier((block, *others))[0]


def in_hbm(block):
    return pltpu.with_memory_space_constraint(block, pltpu.HBM)


def to_core(block):
    return move(block, lambda z, x, y, c: (z, x, y, 1 - c))


def to_y(block, d):
    return move(block, lambda z, x, y, c: (z, x, y + d, c))


def to_x(block, mask):
    return move(block, lambda z, x, y, c: (z, x ^ mask, y, c))


def to_z(block, mask):
    return move(block, lambda z, x, y, c: (z ^ mask, x, y, c))


def dot(a, b):
    return jnp.dot(a, b, preferred_element_type=F32)


def split(a):
    upper = a.astype(BF)
    return upper, (a - upper.astype(F32)).astype(BF)


def dot_16_32(a, b):
    upper, lower = split(b)
    return dot(a, upper) + dot(a, lower)


def dot_32_32(a, b):
    a_upper, a_lower = split(a)
    b_upper, b_lower = split(b)
    return dot(a_upper, b_upper) + (dot(a_upper, b_lower) + dot(a_lower, b_upper))


def kernel_call(body, out_shape, n_scalar, n_in, scratch=(), name=None):
    smem = pl.BlockSpec(memory_space=pltpu.SMEM)
    vmem = pl.BlockSpec(memory_space=pltpu.VMEM)
    outs = out_shape if isinstance(out_shape, (tuple, list)) else (out_shape,)
    out_specs = [vmem] * len(outs)
    return pl.pallas_call(
        body,
        out_shape=out_shape,
        in_specs=[smem] * n_scalar + [vmem] * n_in,
        out_specs=out_specs if isinstance(out_shape, (tuple, list)) else vmem,
        scratch_shapes=list(scratch),
        compiler_params=pltpu.CompilerParams(vmem_limit_bytes=VMEM_LIMIT),
        name=name,
    )


def side_bits(upper, own, sib):
    return jnp.where(upper, sib, own), jnp.where(upper, own, sib)


def live_rhs_body(scalar_ref, rhs_hbm, mine_ref, theirs_ref, rhs_ref, sems):
    first, c = scalar_ref[0], scalar_ref[1]
    rows, half = mine_ref.shape
    tiles = sems.shape[0]
    tile = rows // tiles
    spans = [pl.ds(i * tile, tile) for i in range(tiles)]
    loads = [
        pltpu.make_async_copy(rhs_hbm.at[at], rhs_ref.at[at], sems.at[i])
        for i, at in enumerate(spans)
    ]
    for load in loads:
        load.start()
    iota = lax.broadcasted_iota(jnp.int32, (tile, 1), 0)
    for i, (load, at) in enumerate(zip(loads, spans)):
        load.wait()
        live = first + i * tile + iota < scalar_ref[2]
        for ref, core in ((mine_ref, c), (theirs_ref, 1 - c)):
            part = rhs_ref[at, pl.ds(pl.multiple_of(core * half, half), half)]
            ref[at, :] = jnp.where(live, part, 0.0).astype(BF)


def live_rhs(scalars, rhs):
    rows, columns = rhs.shape
    vmem = pl.BlockSpec(memory_space=pltpu.VMEM)
    out = jax.ShapeDtypeStruct((rows, columns // C), BF)
    return pl.pallas_call(
        live_rhs_body,
        out_shape=(out, out),
        in_specs=[pl.BlockSpec(memory_space=pltpu.SMEM), pl.BlockSpec(memory_space=pltpu.HBM)],
        out_specs=(vmem, vmem),
        scratch_shapes=[pltpu.VMEM(rhs.shape, F32), pltpu.SemaphoreType.DMA((4,))],
        compiler_params=pltpu.CompilerParams(vmem_limit_bytes=VMEM_LIMIT),
        name="live_rhs",
    )(scalars, rhs)


def chip_body(scalar_ref, mine_ref, other_ref, chip_ref):
    c = scalar_ref[1]
    rows = mine_ref.shape[0]
    for ref, core in ((mine_ref, c), (other_ref, 1 - c)):
        chip_ref[pl.ds(pl.multiple_of(core * rows, rows), rows), :] = ref[...]


def halves_body(before_ref, behind_ref, top_ref, bottom_ref):
    rows = top_ref.shape[0]
    top_ref[...] = before_ref[:rows]
    bottom_ref[...] = behind_ref[rows:]


def prepare_body(
    scalar_ref,
    u_hbm,
    v_hbm,
    vt_ref,
    mine_ref,
    theirs_ref,
    u_ref,
    v_ref,
    rows_ref,
    cap_ref,
    sems,
):
    loads = [
        pltpu.make_async_copy(u_hbm, u_ref, sems.at[0]),
        pltpu.make_async_copy(v_hbm, v_ref, sems.at[1]),
    ]
    for load in loads:
        load.start()
    rows = u_ref.shape[1]
    first, c = scalar_ref[0], scalar_ref[1]
    live = first + lax.broadcasted_iota(jnp.int32, (rows, 1), 0) < scalar_ref[2]
    loads[0].wait()
    for l in range(LEVELS):
        rows_ref[:, l * R : (l + 1) * R] = jnp.where(live, u_ref[l].astype(F32), 0.0).astype(BF)
    loads[1].wait()
    for l in range(LEVELS):
        vt_ref[l * R : (l + 1) * R, :] = v_ref[l].T
    for l in range(LEVELS):
        cap = dot(vt_ref[l * R : (l + 1) * R, :], rows_ref[:, : (l + 1) * R])
        for m in range(l + 1):
            cap_ref[FIRST[m] + l - m] = cap[:, m * R : (m + 1) * R]
    half = R // 2
    mine_ref[...] = cap_ref[:, pl.ds(pl.multiple_of(c * half, half), half), :]
    theirs_ref[...] = cap_ref[:, pl.ds(pl.multiple_of((1 - c) * half, half), half), :]


def prepare(scalars, u, v):
    levels, rows, _ = u.shape
    half = jax.ShapeDtypeStruct((N_CAP, R // 2, R), F32)
    hbm = pl.BlockSpec(memory_space=pltpu.HBM)
    vmem = pl.BlockSpec(memory_space=pltpu.VMEM)
    return pl.pallas_call(
        prepare_body,
        out_shape=(
            jax.ShapeDtypeStruct((levels * R, rows), BF),
            half,
            half,
        ),
        in_specs=[pl.BlockSpec(memory_space=pltpu.SMEM), hbm, hbm],
        out_specs=(vmem, vmem, vmem),
        scratch_shapes=[
            pltpu.VMEM(u.shape, BF),
            pltpu.VMEM(v.shape, BF),
            pltpu.VMEM((rows, levels * R), BF),
            pltpu.VMEM((N_CAP, R, R), F32),
            pltpu.SemaphoreType.DMA((2,)),
        ],
        compiler_params=pltpu.CompilerParams(vmem_limit_bytes=VMEM_LIMIT),
        name="prepare",
    )(scalars, u, v)


def cap_parts_body(scalar_ref, mine_ref, other_ref, own_ref, *send_refs):
    y = scalar_ref[3]
    part = own_ref.shape[1]

    def at(d):
        return pl.ds(pl.multiple_of(((y + d) & (Y - 1)) * part, part), part)

    own_ref[...] = mine_ref[:, at(0), :] + other_ref[:, at(0), :]
    for d, ref in enumerate(send_refs):
        ref[...] = (mine_ref[:, at(d + 1), :] + other_ref[:, at(d + 1), :]).astype(BF)


def cap_leaf_body(own_ref, r1_ref, r2_ref, r3_ref, leaf_ref):
    leaf_ref[...] = (own_ref[...] + r1_ref[...].astype(F32)) + (
        r2_ref[...].astype(F32) + r3_ref[...].astype(F32)
    )


def cap_x_body(leaf_ref, r1_ref, r2_ref, r3_ref, low_ref, quad_ref):
    n0, n1 = FIRST[1], FIRST[2]
    low_ref[0, :n0] = leaf_ref[:n0].astype(BF)
    low_ref[1, :n0] = r1_ref[:n0].astype(BF)
    low_ref[0, n0:] = (leaf_ref[n0:n1] + r1_ref[n0:n1]).astype(BF)
    low_ref[1, n0:] = (r2_ref[n0:n1] + r3_ref[n0:n1]).astype(BF)
    quad = ((leaf_ref[n1:] + r1_ref[n1:]) + (r2_ref[n1:] + r3_ref[n1:])).astype(BF)
    for z in range(Z):
        quad_ref[z] = quad


def cap_both_body(z_ref, low_ref, quads_ref, both_ref):
    n0, n1 = FIRST[3] - FIRST[2], FIRST[4] - FIRST[2]
    quads = [quads_ref[z_ref[0] ^ k].astype(F32) for k in range(Z)]
    pairs = [quads[k][n0:] + quads[k + 1][n0:] for k in range(0, Z, 2)]
    fours = [pairs[k][n1 - n0 :] + pairs[k + 1][n1 - n0 :] for k in (0, 2)]
    for side in range(2):
        at = side * N_CAP
        both_ref[at : at + FIRST[2]] = low_ref[side]
        both_ref[at + FIRST[2] : at + FIRST[3]] = quads[side][:n0].astype(BF)
        both_ref[at + FIRST[3] : at + FIRST[4]] = pairs[side][: n1 - n0].astype(BF)
        both_ref[at + FIRST[4] : at + N_CAP] = fours[side].astype(BF)


def cap_stack_body(scalar_ref, b0_ref, b1_ref, b2_ref, b3_ref, out_ref):
    part = b0_ref.shape[1]
    for d, ref in enumerate((b0_ref, b1_ref, b2_ref, b3_ref)):
        at = ((scalar_ref[3] + d) & (Y - 1)) * part
        out_ref[:, pl.ds(pl.multiple_of(at, part), part), :] = ref[...]


def elimination_body(scalar_ref, side_ref, mine_ref, other_ref, g_ref, h_ref, diag_ref, all_ref):
    c = scalar_ref[1]
    half = R // 2
    all_ref[:, pl.ds(pl.multiple_of(c * half, half), half), :] = mine_ref[...]
    all_ref[:, pl.ds(pl.multiple_of((1 - c) * half, half), half), :] = other_ref[...]
    rows = lax.broadcasted_iota(jnp.int32, (R, R), 0)
    cols = lax.broadcasted_iota(jnp.int32, (R, R), 1)
    eye = (rows == cols).astype(F32)
    for m in range(LEVELS):
        upper = side_ref[m] == 1
        first = FIRST[m]
        c0, c1 = side_bits(upper, all_ref[first], all_ref[N_CAP + first])
        diag_ref[m, 0] = c0
        diag_ref[m, 1] = c1
        if m == LEVELS - 1:
            break
        g = g_ref[m]
        g_hi, g_lo = split(g)
        gc0 = dot(g_hi, c0) + dot(g_lo, c0)
        m1 = jnp.where(upper, -gc0, g)
        m0 = jnp.where(upper, eye, 0.0) - dot_16_32(c1, m1)
        m0_hi, m0_lo = split(m0)
        m1_hi, m1_lo = split(m1)
        for l in range(m + 1, LEVELS):
            j = first + l - m
            a0, a1 = side_bits(upper, all_ref[j], all_ref[N_CAP + j])
            h = dot(a0, m0_hi) + dot(a0, m0_lo) + dot(a1, m1_hi) + dot(a1, m1_lo)
            hi, lo = split(h)
            at = (H_FIRST[m] + l - m - 1) * R
            h_ref[at : at + R, 0:R] = hi
            h_ref[at : at + R, R : 2 * R] = lo


def leaf_body(
    chip_ref, a0_hbm, a1_hbm, b0_ref, b1_ref, b2_ref, sum0, sum1, far0, far1, buffers, sems
):
    depth = b0_ref.shape[0]
    loads = []
    for k in range(Y):
        at = pl.ds(pl.multiple_of(chip_ref[k] * depth, depth), depth)
        for i, (a_hbm, far) in enumerate(((a0_hbm, far0), (a1_hbm, far1))):
            to = far if k == Y - 1 else buffers.at[k, i]
            loads.append(pltpu.make_async_copy(a_hbm.at[:, at], to, sems.at[k, i]))
    for load in loads:
        load.start()
    for k, block in enumerate((b0_ref, b1_ref, b2_ref)):
        for i, total in enumerate((sum0, sum1)):
            loads[2 * k + i].wait()
            new = dot(buffers[k, i], block[...])
            total[...] = new if k == 0 else total[...] + new
    for load in loads[2 * (Y - 1) :]:
        load.wait()


def leaf(chips, a_own, a_oth, blocks):
    rows = a_own.shape[0]
    depth, half = blocks[0].shape
    vmem = pl.BlockSpec(memory_space=pltpu.VMEM)
    hbm = pl.BlockSpec(memory_space=pltpu.HBM)
    out_shape = [jax.ShapeDtypeStruct((rows, half), F32)] * 2
    out_shape += [jax.ShapeDtypeStruct((rows, depth), BF)] * 2
    return pl.pallas_call(
        leaf_body,
        out_shape=out_shape,
        in_specs=[pl.BlockSpec(memory_space=pltpu.SMEM), hbm, hbm] + [vmem] * 3,
        out_specs=[vmem] * 4,
        scratch_shapes=[
            pltpu.VMEM((Y - 1, 2, rows, depth), BF),
            pltpu.SemaphoreType.DMA((Y, 2)),
        ],
        compiler_params=pltpu.CompilerParams(vmem_limit_bytes=VMEM_LIMIT),
        name="leaf",
    )(jnp.stack(chips), a_own, a_oth, *blocks)


def project(block, y_refs, v_refs):
    at = pl.ds(pl.multiple_of((block & (Y - 1)) * R, R), R)
    q = None
    for y_ref, v_ref in zip(y_refs, v_refs):
        hi, lo = split(y_ref[:, at])
        new = dot(v_ref[...], jnp.concatenate([hi, lo], axis=1))
        q = new if q is None else q + new
    return (q[:, :R] + q[:, R:]).astype(BF)


def leaf_end_body(
    scalar_ref, a0_ref, a1_ref, top_ref, bottom_ref, sum0_ref, sum1_ref, va_ref, vb_ref, *out_refs
):
    y_refs, q_refs = out_refs[:2], out_refs[2:]
    rows = y_refs[0].shape[0]
    y, c, size = scalar_ref[0], scalar_ref[1], scalar_ref[2]
    iota = lax.broadcasted_iota(jnp.int32, (rows, 1), 0)
    far = jnp.concatenate([top_ref[...], bottom_ref[...]], axis=0)
    for a_ref, sum_ref, y_ref, core in zip(
        (a0_ref, a1_ref), (sum0_ref, sum1_ref), y_refs, (c, 1 - c)
    ):
        new = dot(a_ref[...], far)
        live = (y * C + core) * rows + iota < size
        y_ref[...] = jnp.where(live, sum_ref[...] + new, 0.0)
    for d, q_ref in enumerate(q_refs):
        q_ref[...] = project(y + d + 1, y_refs, (va_ref, vb_ref))


def project_own_body(place_ref, y0_ref, y1_ref, va_ref, vb_ref, q_ref):
    q_ref[...] = project(place_ref[0], (y0_ref, y1_ref), (va_ref, vb_ref))


def eliminate_body(q0_ref, q1_ref, q2_ref, q3_ref, h_ref, e_ref, upper_ref):
    q = (q0_ref[...].astype(F32) + q1_ref[...].astype(F32)) + (
        q2_ref[...].astype(F32) + q3_ref[...].astype(F32)
    )
    for m in range(LEVELS):
        e = q[:R].astype(BF)
        e_ref[m * R : (m + 1) * R, :] = e
        if m > 0:
            upper_ref[(m - 1) * R : m * R, :] = e
        if m < LEVELS - 1:
            at, n = H_FIRST[m] * R, (LEVELS - 1 - m) * R
            q = q[R:] - dot(h_ref[at : at + n, :], jnp.concatenate([e, e], axis=0))


def solve(c0, c1, upper, own, sib, g):
    s0, s1 = side_bits(upper, own, sib)
    inner = s0 - dot_16_32(c0, s1)
    t1 = dot_32_32(g, inner)
    t0 = s1 - dot_16_32(c1, t1)
    return jnp.where(upper, t1, t0)


def solve_two_body(levels, side_ref, diag_ref, g_ref, a_ref, r1_ref, r2_ref, r3_ref, t_ref):
    low, high = levels
    one = slice(0, R)
    two = slice(R, 2 * R)
    t = solve(
        diag_ref[low, 0],
        diag_ref[low, 1],
        side_ref[low] == 1,
        a_ref[one].astype(F32),
        r1_ref[one].astype(F32),
        g_ref[low],
    )
    t_ref[one] = t.astype(BF)
    t = solve(
        diag_ref[high, 0],
        diag_ref[high, 1],
        side_ref[high] == 1,
        a_ref[two].astype(F32) + r1_ref[two].astype(F32),
        r2_ref[one].astype(F32) + r3_ref[one].astype(F32),
        g_ref[high],
    )
    t_ref[two] = t.astype(BF)


def quad_body(e_ref, r1_ref, r2_ref, r3_ref, quad_ref, upper_ref):
    two = slice(2 * R, 5 * R)
    quad = e_ref[two].astype(F32) + r1_ref[two].astype(F32)
    quad = quad + (r2_ref[R:].astype(F32) + r3_ref[R:].astype(F32))
    quad = quad.astype(BF)
    quad_ref[...] = quad
    upper_ref[...] = quad[R:]


def own4_body(quad_ref, z1_ref, z2_ref, z3_ref, own_ref):
    own = quad_ref[2 * R :].astype(F32) + z1_ref[2 * R :].astype(F32)
    own_ref[...] = (own + (z2_ref[R:].astype(F32) + z3_ref[R:].astype(F32))).astype(BF)


def solve_last_body(side_ref, diag_ref, g_ref, a_ref, r_ref, t01_ref, t23_ref, t_ref):
    last = LEVELS - 1
    t = solve(
        diag_ref[last, 0],
        diag_ref[last, 1],
        side_ref[last] == 1,
        a_ref[...].astype(F32),
        r_ref[...].astype(F32),
        g_ref[last],
    )
    t_ref[: 2 * R] = t01_ref[...]
    t_ref[2 * R : 4 * R] = t23_ref[...]
    t_ref[4 * R :] = t.astype(BF)


def columns_body(y_ref, b0_ref, b1_ref, b2_ref, b3_ref, out_ref):
    for d, ref in enumerate((b0_ref, b1_ref, b2_ref, b3_ref)):
        at = ((y_ref[0] + d) & (Y - 1)) * R
        out_ref[:, pl.ds(pl.multiple_of(at, R), R)] = ref[...]


def gather_y(block):
    return [block, to_y(block, -1), to_y(block, 2), to_y(block, 1)]


def put_columns(y, blocks):
    out = jax.ShapeDtypeStruct((blocks[0].shape[0], Y * R), BF)
    return kernel_call(columns_body, out, 1, Y, name="columns")(y[None], *blocks)


def bring_body(*refs):
    n = (len(refs) - 1) // 2
    sems = refs[-1]
    copies = [
        pltpu.make_async_copy(refs[i], refs[n + i], sems.at[i]) for i in range(n)
    ]
    for copy in copies:
        copy.start()
    for copy in copies:
        copy.wait()


def bring(*arrays):
    n = len(arrays)
    size = sum(a.size * a.dtype.itemsize for a in arrays)
    return pl.pallas_call(
        bring_body,
        out_shape=[jax.ShapeDtypeStruct(a.shape, a.dtype) for a in arrays],
        in_specs=[pl.BlockSpec(memory_space=pltpu.HBM)] * n,
        out_specs=[pl.BlockSpec(memory_space=pltpu.VMEM)] * n,
        scratch_shapes=[pltpu.SemaphoreType.DMA((n,))],
        compiler_params=pltpu.CompilerParams(vmem_limit_bytes=VMEM_LIMIT),
        cost_estimate=pl.CostEstimate(flops=0, bytes_accessed=2 * size, transcendentals=0),
        name="bring",
    )(*[in_hbm(a) for a in arrays])


def update_body(scalar_ref, y0_ref, y1_ref, u_ref, t0_ref, t1_ref, out_hbm, held, sems):
    rows, half = y0_ref.shape
    tiles = sems.shape[0]
    tile = rows // tiles
    first, c, size = scalar_ref[0], scalar_ref[1], scalar_ref[2]
    iota = lax.broadcasted_iota(jnp.int32, (tile, 1), 0)
    copies = []
    for i in range(tiles):
        at_row = pl.ds(i * tile, tile)
        u = jnp.concatenate([u_ref[l, at_row, :] for l in range(LEVELS)], axis=1)
        live = first + i * tile + iota < size
        for y_ref, t_ref, core in ((y0_ref, t0_ref, c), (y1_ref, t1_ref, 1 - c)):
            at = pl.ds(pl.multiple_of(core * half, half), half)
            held[at_row, at] = y_ref[at_row, :] - jnp.where(live, dot(u, t_ref[...]), 0.0)
        copy = pltpu.make_async_copy(held.at[at_row], out_hbm.at[at_row], sems.at[i])
        copy.start()
        copies.append(copy)
    for copy in copies:
        copy.wait()


def update(scalars, y_own, y_oth, u, t_own, t_oth):
    rows, half = y_own.shape
    vmem = pl.BlockSpec(memory_space=pltpu.VMEM)
    return pl.pallas_call(
        update_body,
        out_shape=jax.ShapeDtypeStruct((rows, 2 * half), F32),
        in_specs=[pl.BlockSpec(memory_space=pltpu.SMEM)] + [vmem] * 5,
        out_specs=pl.BlockSpec(memory_space=pl.ANY),
        scratch_shapes=[pltpu.VMEM((rows, 2 * half), F32), pltpu.SemaphoreType.DMA((4,))],
        compiler_params=pltpu.CompilerParams(vmem_limit_bytes=VMEM_LIMIT),
        name="update",
    )(scalars, y_own, y_oth, u, t_own, t_oth)


def shards(rhs, leaf_inverse, leaf_sizes, u_tilde, v_right, cap_factor):
    rows, columns = rhs.shape
    row = lax.axis_index("row").astype(jnp.int32)
    partner = lax.axis_index("partner").astype(jnp.int32)
    y, c = row >> 1, row & 1
    side = (partner >> jnp.arange(LEVELS, dtype=jnp.int32)) & 1
    scalars = jnp.stack([row * rows, c, leaf_sizes[0], y])
    g = cap_factor[:, 0]
    struct = jax.ShapeDtypeStruct

    part_shape = struct((rows, columns // C), BF)
    mine, theirs = live_rhs(scalars, in_hbm(rhs))
    other = to_core(theirs)

    half, part = R // 2, R // C // Y
    vt, cap_mine, cap_theirs = prepare(scalars, in_hbm(u_tilde), in_hbm(v_right))
    part_struct = struct((N_CAP, part, R), BF)
    own, s1, s2, s3 = kernel_call(
        cap_parts_body,
        (struct((N_CAP, part, R), F32), part_struct, part_struct, part_struct),
        1,
        2,
        name="cap_parts",
    )(scalars, cap_mine, to_core(cap_theirs))
    part1, part2, part3 = to_y(s1, 1), to_y(s2, 2), to_y(s3, 3)

    a_oth = to_core(after(leaf_inverse, own))
    vt_oth = to_core(after(vt, own))
    chip = kernel_call(
        chip_body, struct((C * rows, columns // C), BF), 1, 2, name="chip"
    )(scalars, after(mine, part1, vt_oth), other)
    before, behind = to_y(chip, 1), to_y(after(chip, part2, part3, a_oth), -1)
    cap_leaf = kernel_call(cap_leaf_body, struct((N_CAP, part, R), F32), 0, 4, name="cap_leaf")(
        own, part1, part2, part3
    )
    n_high = N_CAP - FIRST[2]
    low, cap_quad = kernel_call(
        cap_x_body,
        (struct((2, FIRST[2], part, R), BF), struct((Z, n_high, part, R), BF)),
        0,
        4,
        name="cap_x",
    )(cap_leaf, to_x(cap_leaf, 1), to_x(cap_leaf, 2), to_x(cap_leaf, 3))
    cap_quads = lax.all_to_all(
        cap_quad,
        "partner",
        0,
        0,
        axis_index_groups=[[z * X + x for z in range(Z)] for x in range(X)],
    )
    both = kernel_call(
        cap_both_body, struct((2 * N_CAP, part, R), BF), 1, 2, name="cap_both"
    )((partner >> 2)[None], low, cap_quads)
    top, bottom = kernel_call(
        halves_body, (part_shape, part_shape), 0, 2, name="halves"
    )(after(before, both), behind)
    far_top, far_bottom = to_y(top, 1), to_y(bottom, -1)
    places = jnp.stack([y, c, leaf_sizes[0]])
    along = [(y + d) & (Y - 1) for d in range(Y)]
    sum_own, sum_oth, far_own, far_oth = leaf(
        [along[0], along[3], along[1], along[2]],
        in_hbm(leaf_inverse),
        in_hbm(a_oth),
        [chip, before, behind],
    )
    both = after(both, top)
    cap_rows = kernel_call(
        cap_stack_body, struct((2 * N_CAP, half, R), BF), 1, 4, name="cap_stack"
    )(scalars, *gather_y(both))
    h, diag = kernel_call(
        elimination_body,
        (struct((N_H * R, 2 * R), BF), struct((LEVELS, 2, R, R), BF)),
        2,
        3,
        scratch=[pltpu.VMEM((2 * N_CAP, R, R), BF)],
        name="elimination",
    )(scalars, side, cap_rows, to_core(cap_rows), g)

    places = after(places, cap_rows)
    y_own, y_oth, *q = kernel_call(
        leaf_end_body,
        [struct((rows, columns // C), F32)] * 2 + [struct((LEVELS * R, R), BF)] * (Y - 1),
        1,
        8,
        name="leaf_end",
    )(places, far_own, far_oth, far_top, far_bottom, sum_own, sum_oth, vt, vt_oth)
    q_own = kernel_call(
        project_own_body, struct((LEVELS * R, R), BF), 1, 4, name="project_own"
    )(places, y_own, y_oth, vt, vt_oth)
    y_other = to_core(y_oth)

    e, e_up = kernel_call(
        eliminate_body,
        (struct((LEVELS * R, R), BF), struct(((LEVELS - 1) * R, R), BF)),
        0,
        5,
        name="eliminate",
    )(q_own, to_y(q[0], 1), to_y(q[1], 2), to_y(q[2], 3), after(h, y_other))
    two = struct((2 * R, R), BF)
    r1, r2, r3 = to_x(e, 1), to_x(e_up, 2), to_x(e_up, 3)
    quad, quad_up = kernel_call(
        quad_body, (struct((3 * R, R), BF), struct((2 * R, R), BF)), 0, 4, name="quad"
    )(e, r1, r2, r3)
    z1, z2, z3 = to_z(quad, 1), to_z(quad_up, 2), to_z(quad_up, 3)
    t01 = kernel_call(
        lambda *refs: solve_two_body((0, 1), *refs), two, 1, 6, name="solve_0_1"
    )(side, diag, g, after(e, quad), r1, r2, r3)
    own4 = kernel_call(own4_body, struct((R, R), BF), 0, 4, name="own4")(
        after(quad, t01), z1, z2, z3
    )
    sib4 = to_z(own4, 4)
    t23 = kernel_call(
        lambda *refs: solve_two_body((2, 3), *refs), two, 1, 6, name="solve_2_3"
    )(side, diag, g, after(quad, own4), z1, z2, z3)
    t = kernel_call(solve_last_body, struct((LEVELS * R, R), BF), 1, 6, name="solve_4")(
        side, diag, g, own4, sib4, t01, t23
    )
    t_own = put_columns(y, gather_y(t))
    t_oth = to_core(t_own)
    return update(scalars, *bring(y_own, y_other, u_tilde), t_own, t_oth)


def solution(mesh):
    return jax.shard_map(
        shards,
        mesh=mesh,
        in_specs=(
            P(("partner", "row"), None),
            P(("partner", "row"), None),
            P("partner"),
            P(None, ("partner", "row"), None),
            P(None, ("partner", "row"), None),
            P(None, "partner", None, None),
        ),
        out_specs=P(("partner", "row"), None),
        check_vma=False,
    )
```

```python
import jax
import jax.numpy as jnp
from jax import lax
from jax.experimental import pallas as pl
from jax.experimental.pallas import tpu as pltpu
from jax.sharding import PartitionSpec as P

Z, X, Y, C = 8, 4, 4, 2
LEVELS = 5
R = 128
BF = jnp.bfloat16
F32 = jnp.float32
FIRST = (0, 5, 9, 12, 14)
N_CAP = 15
H_FIRST = (0, 4, 7, 9)
N_H = 10
VMEM_LIMIT = 16 * 1024 * 1024


def move(block, where):
    route = []
    for z in range(Z):
        for x in range(X):
            for y in range(Y):
                for c in range(C):
                    z1, x1, y1, c1 = where(z, x, y, c)
                    here = ((z * X + x) * Y + y) * C + c
                    there = ((z1 % Z * X + x1 % X) * Y + y1 % Y) * C + c1 % C
                    route.append((here, there))
    return lax.ppermute(block, ("partner", "row"), route)


def after(block, *others):
    return lax.optimization_barrier((block, *others))[0]


def in_hbm(block):
    return pltpu.with_memory_space_constraint(block, pltpu.HBM)


def to_core(block):
    return move(block, lambda z, x, y, c: (z, x, y, 1 - c))


def to_y(block, d):
    return move(block, lambda z, x, y, c: (z, x, y + d, c))


def to_x(block, mask):
    return move(block, lambda z, x, y, c: (z, x ^ mask, y, c))


def to_z(block, mask):
    return move(block, lambda z, x, y, c: (z ^ mask, x, y, c))


def dot(a, b):
    return jnp.dot(a, b, preferred_element_type=F32)


def split(a):
    upper = a.astype(BF)
    return upper, (a - upper.astype(F32)).astype(BF)


def dot_16_32(a, b):
    upper, lower = split(b)
    return dot(a, upper) + dot(a, lower)


def dot_32_32(a, b):
    a_upper, a_lower = split(a)
    b_upper, b_lower = split(b)
    return dot(a_upper, b_upper) + (dot(a_upper, b_lower) + dot(a_lower, b_upper))


def cost(microseconds):
    return pl.CostEstimate(
        flops=int(microseconds * 1.1e9), bytes_accessed=int(microseconds * 1e6), transcendentals=0
    )


def kernel_call(body, out_shape, n_scalar, n_in, scratch=(), name=None, us=None):
    smem = pl.BlockSpec(memory_space=pltpu.SMEM)
    vmem = pl.BlockSpec(memory_space=pltpu.VMEM)
    outs = out_shape if isinstance(out_shape, (tuple, list)) else (out_shape,)
    out_specs = [vmem] * len(outs)
    return pl.pallas_call(
        body,
        out_shape=out_shape,
        in_specs=[smem] * n_scalar + [vmem] * n_in,
        out_specs=out_specs if isinstance(out_shape, (tuple, list)) else vmem,
        scratch_shapes=list(scratch),
        compiler_params=pltpu.CompilerParams(vmem_limit_bytes=VMEM_LIMIT),
        cost_estimate=None if us is None else cost(us),
        name=name,
    )


def side_bits(upper, own, sib):
    return jnp.where(upper, sib, own), jnp.where(upper, own, sib)


def live_rhs_body(scalar_ref, rhs_hbm, mine_ref, theirs_ref, rhs_ref, sems):
    first, c = scalar_ref[0], scalar_ref[1]
    rows, half = mine_ref.shape
    tiles = sems.shape[0]
    tile = rows // tiles
    spans = [pl.ds(i * tile, tile) for i in range(tiles)]
    loads = [
        pltpu.make_async_copy(rhs_hbm.at[at], rhs_ref.at[at], sems.at[i])
        for i, at in enumerate(spans)
    ]
    for load in loads:
        load.start()
    iota = lax.broadcasted_iota(jnp.int32, (tile, 1), 0)
    for i, (load, at) in enumerate(zip(loads, spans)):
        load.wait()
        live = first + i * tile + iota < scalar_ref[2]
        for ref, core in ((mine_ref, c), (theirs_ref, 1 - c)):
            part = rhs_ref[at, pl.ds(pl.multiple_of(core * half, half), half)]
            ref[at, :] = jnp.where(live, part, 0.0).astype(BF)


def live_rhs(scalars, rhs):
    rows, columns = rhs.shape
    vmem = pl.BlockSpec(memory_space=pltpu.VMEM)
    out = jax.ShapeDtypeStruct((rows, columns // C), BF)
    return pl.pallas_call(
        live_rhs_body,
        out_shape=(out, out),
        in_specs=[pl.BlockSpec(memory_space=pltpu.SMEM), pl.BlockSpec(memory_space=pltpu.HBM)],
        out_specs=(vmem, vmem),
        scratch_shapes=[pltpu.VMEM(rhs.shape, F32), pltpu.SemaphoreType.DMA((4,))],
        compiler_params=pltpu.CompilerParams(vmem_limit_bytes=VMEM_LIMIT),
        name="live_rhs",
    )(scalars, rhs)


def chip_body(scalar_ref, mine_ref, other_ref, chip_ref):
    c = scalar_ref[1]
    rows = mine_ref.shape[0]
    for ref, core in ((mine_ref, c), (other_ref, 1 - c)):
        chip_ref[pl.ds(pl.multiple_of(core * rows, rows), rows), :] = ref[...]


def halves_body(before_ref, behind_ref, top_ref, bottom_ref):
    rows = top_ref.shape[0]
    top_ref[...] = before_ref[:rows]
    bottom_ref[...] = behind_ref[rows:]


def prepare_body(
    scalar_ref,
    u_hbm,
    v_hbm,
    vt_ref,
    mine_ref,
    theirs_ref,
    u_ref,
    v_ref,
    rows_ref,
    cap_ref,
    sems,
):
    loads = [
        pltpu.make_async_copy(u_hbm, u_ref, sems.at[0]),
        pltpu.make_async_copy(v_hbm, v_ref, sems.at[1]),
    ]
    for load in loads:
        load.start()
    rows = u_ref.shape[1]
    first, c = scalar_ref[0], scalar_ref[1]
    live = first + lax.broadcasted_iota(jnp.int32, (rows, 1), 0) < scalar_ref[2]
    loads[0].wait()
    for l in range(LEVELS):
        rows_ref[:, l * R : (l + 1) * R] = jnp.where(live, u_ref[l].astype(F32), 0.0).astype(BF)
    loads[1].wait()
    for l in range(LEVELS):
        vt_ref[l * R : (l + 1) * R, :] = v_ref[l].T
    for l in range(LEVELS):
        cap = dot(vt_ref[l * R : (l + 1) * R, :], rows_ref[:, : (l + 1) * R])
        for m in range(l + 1):
            cap_ref[FIRST[m] + l - m] = cap[:, m * R : (m + 1) * R]
    half = R // 2
    mine_ref[...] = cap_ref[:, pl.ds(pl.multiple_of(c * half, half), half), :]
    theirs_ref[...] = cap_ref[:, pl.ds(pl.multiple_of((1 - c) * half, half), half), :]


def prepare(scalars, u, v):
    levels, rows, _ = u.shape
    half = jax.ShapeDtypeStruct((N_CAP, R // 2, R), F32)
    hbm = pl.BlockSpec(memory_space=pltpu.HBM)
    vmem = pl.BlockSpec(memory_space=pltpu.VMEM)
    return pl.pallas_call(
        prepare_body,
        out_shape=(
            jax.ShapeDtypeStruct((levels * R, rows), BF),
            half,
            half,
        ),
        in_specs=[pl.BlockSpec(memory_space=pltpu.SMEM), hbm, hbm],
        out_specs=(vmem, vmem, vmem),
        scratch_shapes=[
            pltpu.VMEM(u.shape, BF),
            pltpu.VMEM(v.shape, BF),
            pltpu.VMEM((rows, levels * R), BF),
            pltpu.VMEM((N_CAP, R, R), F32),
            pltpu.SemaphoreType.DMA((2,)),
        ],
        compiler_params=pltpu.CompilerParams(vmem_limit_bytes=VMEM_LIMIT),
        name="prepare",
    )(scalars, u, v)


def cap_parts_body(scalar_ref, mine_ref, other_ref, own_ref, *send_refs):
    y = scalar_ref[3]
    part = own_ref.shape[1]

    def at(d):
        return pl.ds(pl.multiple_of(((y + d) & (Y - 1)) * part, part), part)

    own_ref[...] = mine_ref[:, at(0), :] + other_ref[:, at(0), :]
    for d, ref in enumerate(send_refs):
        ref[...] = (mine_ref[:, at(d + 1), :] + other_ref[:, at(d + 1), :]).astype(BF)


def cap_leaf_body(own_ref, r1_ref, r2_ref, r3_ref, leaf_ref, send_ref, upper_ref):
    leaf = (own_ref[...] + r1_ref[...].astype(F32)) + (
        r2_ref[...].astype(F32) + r3_ref[...].astype(F32)
    )
    leaf_ref[...] = leaf
    send_ref[...] = leaf.astype(BF)
    upper_ref[...] = leaf[FIRST[1] :].astype(BF)


def cap_x_body(leaf_ref, r1_ref, r2_ref, r3_ref, low_ref, quad_ref, send_ref, upper_ref):
    n0, n1 = FIRST[1], FIRST[2]
    low_ref[0, :n0] = leaf_ref[:n0].astype(BF)
    low_ref[1, :n0] = r1_ref[:n0]
    low_ref[0, n0:] = (leaf_ref[n0:n1] + r1_ref[n0:n1].astype(F32)).astype(BF)
    other = r2_ref[...].astype(F32) + r3_ref[...].astype(F32)
    low_ref[1, n0:] = other[: n1 - n0].astype(BF)
    quad = (leaf_ref[n1:] + r1_ref[n1:].astype(F32)) + other[n1 - n0 :]
    quad_ref[...] = quad
    send_ref[...] = quad.astype(BF)
    upper_ref[...] = quad[FIRST[3] - n1 :].astype(BF)


def cap_z_body(quad_ref, z1_ref, z2_ref, z3_ref, mid_ref, last_ref):
    n0, n1 = FIRST[3] - FIRST[2], FIRST[4] - FIRST[2]
    other = z2_ref[...].astype(F32) + z3_ref[...].astype(F32)
    mid_ref[0, :n0] = quad_ref[:n0].astype(BF)
    mid_ref[1, :n0] = z1_ref[:n0]
    mid_ref[0, n0:] = (quad_ref[n0:n1] + z1_ref[n0:n1].astype(F32)).astype(BF)
    mid_ref[1, n0:] = other[: n1 - n0].astype(BF)
    last_ref[...] = (quad_ref[n1:] + z1_ref[n1:].astype(F32)) + other[n1 - n0 :]


def cap_both_body(low_ref, mid_ref, own4_ref, sib4_ref, both_ref):
    for side, last_ref in enumerate((own4_ref, sib4_ref)):
        at = side * N_CAP
        both_ref[at : at + FIRST[2]] = low_ref[side]
        both_ref[at + FIRST[2] : at + FIRST[4]] = mid_ref[side]
        both_ref[at + FIRST[4]] = last_ref[0].astype(BF)


def cap_stack_body(scalar_ref, b0_ref, b1_ref, b2_ref, b3_ref, out_ref):
    part = b0_ref.shape[1]
    for d, ref in enumerate((b0_ref, b1_ref, b2_ref, b3_ref)):
        at = ((scalar_ref[3] + d) & (Y - 1)) * part
        out_ref[:, pl.ds(pl.multiple_of(at, part), part), :] = ref[...]


def elimination_body(scalar_ref, side_ref, mine_ref, other_ref, g_ref, h_ref, diag_ref, all_ref):
    c = scalar_ref[1]
    half = R // 2
    all_ref[:, pl.ds(pl.multiple_of(c * half, half), half), :] = mine_ref[...]
    all_ref[:, pl.ds(pl.multiple_of((1 - c) * half, half), half), :] = other_ref[...]
    rows = lax.broadcasted_iota(jnp.int32, (R, R), 0)
    cols = lax.broadcasted_iota(jnp.int32, (R, R), 1)
    eye = (rows == cols).astype(F32)
    for m in range(LEVELS):
        upper = side_ref[m] == 1
        first = FIRST[m]
        c0, c1 = side_bits(upper, all_ref[first], all_ref[N_CAP + first])
        diag_ref[m, 0] = c0
        diag_ref[m, 1] = c1
        if m == LEVELS - 1:
            break
        g = g_ref[m]
        g_hi, g_lo = split(g)
        gc0 = dot(g_hi, c0) + dot(g_lo, c0)
        m1 = jnp.where(upper, -gc0, g)
        m0 = jnp.where(upper, eye, 0.0) - dot_16_32(c1, m1)
        m0_hi, m0_lo = split(m0)
        m1_hi, m1_lo = split(m1)
        for l in range(m + 1, LEVELS):
            j = first + l - m
            a0, a1 = side_bits(upper, all_ref[j], all_ref[N_CAP + j])
            h = dot(a0, m0_hi) + dot(a0, m0_lo) + dot(a1, m1_hi) + dot(a1, m1_lo)
            hi, lo = split(h)
            at = (H_FIRST[m] + l - m - 1) * R
            h_ref[at : at + R, 0:R] = hi
            h_ref[at : at + R, R : 2 * R] = lo


def leaf_body(
    chip_ref, a0_hbm, a1_hbm, b0_ref, b1_ref, b2_ref, sum0, sum1, far0, far1, buffers, sems
):
    depth = b0_ref.shape[0]
    loads = []
    for k in range(Y):
        at = pl.ds(pl.multiple_of(chip_ref[k] * depth, depth), depth)
        for i, (a_hbm, far) in enumerate(((a0_hbm, far0), (a1_hbm, far1))):
            to = far if k == Y - 1 else buffers.at[k, i]
            loads.append(pltpu.make_async_copy(a_hbm.at[:, at], to, sems.at[k, i]))
    for load in loads:
        load.start()
    for k, block in enumerate((b0_ref, b1_ref, b2_ref)):
        for i, total in enumerate((sum0, sum1)):
            loads[2 * k + i].wait()
            new = dot(buffers[k, i], block[...])
            total[...] = new if k == 0 else total[...] + new
    for load in loads[2 * (Y - 1) :]:
        load.wait()


def leaf(chips, a_own, a_oth, blocks):
    rows = a_own.shape[0]
    depth, half = blocks[0].shape
    vmem = pl.BlockSpec(memory_space=pltpu.VMEM)
    hbm = pl.BlockSpec(memory_space=pltpu.HBM)
    out_shape = [jax.ShapeDtypeStruct((rows, half), F32)] * 2
    out_shape += [jax.ShapeDtypeStruct((rows, depth), BF)] * 2
    return pl.pallas_call(
        leaf_body,
        out_shape=out_shape,
        in_specs=[pl.BlockSpec(memory_space=pltpu.SMEM), hbm, hbm] + [vmem] * 3,
        out_specs=[vmem] * 4,
        scratch_shapes=[
            pltpu.VMEM((Y - 1, 2, rows, depth), BF),
            pltpu.SemaphoreType.DMA((Y, 2)),
        ],
        compiler_params=pltpu.CompilerParams(vmem_limit_bytes=VMEM_LIMIT),
        name="leaf",
    )(jnp.stack(chips), a_own, a_oth, *blocks)


def project(blocks, y_refs, v_refs, q_refs):
    q = None
    for y_ref, v_ref in zip(y_refs, v_refs):
        parts = []
        for block in blocks:
            at = pl.ds(pl.multiple_of((block & (Y - 1)) * R, R), R)
            parts.append(y_ref[:, at].astype(BF))
        new = dot(v_ref[...], parts[0] if len(parts) == 1 else jnp.concatenate(parts, axis=1))
        q = new if q is None else q + new
    for k, q_ref in enumerate(q_refs):
        q_ref[...] = q[:, k * R : (k + 1) * R].astype(BF)


def leaf_end_body(
    scalar_ref, a0_ref, a1_ref, top_ref, bottom_ref, sum0_ref, sum1_ref, va_ref, vb_ref, *out_refs
):
    y_refs, q_refs = out_refs[:2], out_refs[2:]
    rows = y_refs[0].shape[0]
    y, c, size = scalar_ref[0], scalar_ref[1], scalar_ref[2]
    iota = lax.broadcasted_iota(jnp.int32, (rows, 1), 0)
    far = jnp.concatenate([top_ref[...], bottom_ref[...]], axis=0)
    for a_ref, sum_ref, y_ref, core in zip(
        (a0_ref, a1_ref), (sum0_ref, sum1_ref), y_refs, (c, 1 - c)
    ):
        new = dot(a_ref[...], far)
        live = (y * C + core) * rows + iota < size
        y_ref[...] = jnp.where(live, sum_ref[...] + new, 0.0)
    project([y + d + 1 for d in range(len(q_refs))], y_refs, (va_ref, vb_ref), q_refs)


def project_own_body(place_ref, y0_ref, y1_ref, va_ref, vb_ref, q_ref):
    project([place_ref[0]], (y0_ref, y1_ref), (va_ref, vb_ref), [q_ref])


def eliminate_body(q0_ref, q1_ref, q2_ref, q3_ref, h_ref, e_ref, upper_ref):
    q = (q0_ref[...].astype(F32) + q1_ref[...].astype(F32)) + (
        q2_ref[...].astype(F32) + q3_ref[...].astype(F32)
    )
    for m in range(LEVELS):
        e = q[:R].astype(BF)
        e_ref[m * R : (m + 1) * R, :] = e
        if m > 0:
            upper_ref[(m - 1) * R : m * R, :] = e
        if m < LEVELS - 1:
            at, n = H_FIRST[m] * R, (LEVELS - 1 - m) * R
            q = q[R:] - dot(h_ref[at : at + n, :], jnp.concatenate([e, e], axis=0))


def solve(c0, c1, upper, own, sib, g):
    s0, s1 = side_bits(upper, own, sib)
    inner = s0 - dot_16_32(c0, s1)
    t1 = dot_32_32(g, inner)
    t0 = s1 - dot_16_32(c1, t1)
    return jnp.where(upper, t1, t0)


def solve_two_body(levels, side_ref, diag_ref, g_ref, a_ref, r1_ref, r2_ref, r3_ref, t_ref):
    low, high = levels
    one = slice(0, R)
    two = slice(R, 2 * R)
    t = solve(
        diag_ref[low, 0],
        diag_ref[low, 1],
        side_ref[low] == 1,
        a_ref[one].astype(F32),
        r1_ref[one].astype(F32),
        g_ref[low],
    )
    t_ref[one] = t.astype(BF)
    t = solve(
        diag_ref[high, 0],
        diag_ref[high, 1],
        side_ref[high] == 1,
        a_ref[two].astype(F32) + r1_ref[two].astype(F32),
        r2_ref[one].astype(F32) + r3_ref[one].astype(F32),
        g_ref[high],
    )
    t_ref[two] = t.astype(BF)


def quad_body(e_ref, r1_ref, r2_ref, r3_ref, quad_ref, upper_ref):
    two = slice(2 * R, 5 * R)
    quad = e_ref[two].astype(F32) + r1_ref[two].astype(F32)
    quad = quad + (r2_ref[R:].astype(F32) + r3_ref[R:].astype(F32))
    quad = quad.astype(BF)
    quad_ref[...] = quad
    upper_ref[...] = quad[R:]


def own4_body(quad_ref, z1_ref, z2_ref, z3_ref, own_ref):
    own = quad_ref[2 * R :].astype(F32) + z1_ref[2 * R :].astype(F32)
    own_ref[...] = (own + (z2_ref[R:].astype(F32) + z3_ref[R:].astype(F32))).astype(BF)


def solve_last_body(side_ref, diag_ref, g_ref, a_ref, r_ref, t01_ref, t23_ref, t_ref):
    last = LEVELS - 1
    t = solve(
        diag_ref[last, 0],
        diag_ref[last, 1],
        side_ref[last] == 1,
        a_ref[...].astype(F32),
        r_ref[...].astype(F32),
        g_ref[last],
    )
    t_ref[: 2 * R] = t01_ref[...]
    t_ref[2 * R : 4 * R] = t23_ref[...]
    t_ref[4 * R :] = t.astype(BF)


def columns_body(y_ref, b0_ref, b1_ref, b2_ref, b3_ref, out_ref):
    for d, ref in enumerate((b0_ref, b1_ref, b2_ref, b3_ref)):
        at = ((y_ref[0] + d) & (Y - 1)) * R
        out_ref[:, pl.ds(pl.multiple_of(at, R), R)] = ref[...]


def gather_y(block):
    return [block, to_y(block, -1), to_y(block, 2), to_y(block, 1)]


def put_columns(y, blocks):
    out = jax.ShapeDtypeStruct((blocks[0].shape[0], Y * R), BF)
    return kernel_call(columns_body, out, 1, Y, name="columns")(y[None], *blocks)


def bring_body(*refs):
    n = (len(refs) - 1) // 2
    sems = refs[-1]
    copies = [
        pltpu.make_async_copy(refs[i], refs[n + i], sems.at[i]) for i in range(n)
    ]
    for copy in copies:
        copy.start()
    for copy in copies:
        copy.wait()


def bring(*arrays):
    n = len(arrays)
    size = sum(a.size * a.dtype.itemsize for a in arrays)
    return pl.pallas_call(
        bring_body,
        out_shape=[jax.ShapeDtypeStruct(a.shape, a.dtype) for a in arrays],
        in_specs=[pl.BlockSpec(memory_space=pltpu.HBM)] * n,
        out_specs=[pl.BlockSpec(memory_space=pltpu.VMEM)] * n,
        scratch_shapes=[pltpu.SemaphoreType.DMA((n,))],
        compiler_params=pltpu.CompilerParams(vmem_limit_bytes=VMEM_LIMIT),
        cost_estimate=pl.CostEstimate(flops=0, bytes_accessed=2 * size, transcendentals=0),
        name="bring",
    )(*[in_hbm(a) for a in arrays])


def update_body(scalar_ref, y0_ref, y1_ref, u_ref, t0_ref, t1_ref, out_hbm, held, sems):
    rows, half = y0_ref.shape
    tiles = sems.shape[0]
    tile = rows // tiles
    first, c, size = scalar_ref[0], scalar_ref[1], scalar_ref[2]
    iota = lax.broadcasted_iota(jnp.int32, (tile, 1), 0)
    copies = []
    for i in range(tiles):
        at_row = pl.ds(i * tile, tile)
        u = jnp.concatenate([u_ref[l, at_row, :] for l in range(LEVELS)], axis=1)
        live = first + i * tile + iota < size
        for y_ref, t_ref, core in ((y0_ref, t0_ref, c), (y1_ref, t1_ref, 1 - c)):
            at = pl.ds(pl.multiple_of(core * half, half), half)
            held[at_row, at] = y_ref[at_row, :] - jnp.where(live, dot(u, t_ref[...]), 0.0)
        copy = pltpu.make_async_copy(held.at[at_row], out_hbm.at[at_row], sems.at[i])
        copy.start()
        copies.append(copy)
    for copy in copies:
        copy.wait()


def update(scalars, y_own, y_oth, u, t_own, t_oth):
    rows, half = y_own.shape
    vmem = pl.BlockSpec(memory_space=pltpu.VMEM)
    return pl.pallas_call(
        update_body,
        out_shape=jax.ShapeDtypeStruct((rows, 2 * half), F32),
        in_specs=[pl.BlockSpec(memory_space=pltpu.SMEM)] + [vmem] * 5,
        out_specs=pl.BlockSpec(memory_space=pl.ANY),
        scratch_shapes=[pltpu.VMEM((rows, 2 * half), F32), pltpu.SemaphoreType.DMA((4,))],
        compiler_params=pltpu.CompilerParams(vmem_limit_bytes=VMEM_LIMIT),
        name="update",
    )(scalars, y_own, y_oth, u, t_own, t_oth)


def shards(rhs, leaf_inverse, leaf_sizes, u_tilde, v_right, cap_factor):
    rows, columns = rhs.shape
    row = lax.axis_index("row").astype(jnp.int32)
    partner = lax.axis_index("partner").astype(jnp.int32)
    y, c = row >> 1, row & 1
    side = (partner >> jnp.arange(LEVELS, dtype=jnp.int32)) & 1
    scalars = jnp.stack([row * rows, c, leaf_sizes[0], y])
    g = cap_factor[:, 0]
    struct = jax.ShapeDtypeStruct

    part_shape = struct((rows, columns // C), BF)
    mine, theirs = live_rhs(scalars, in_hbm(rhs))
    other = to_core(theirs)

    half, part = R // 2, R // C // Y
    vt, cap_mine, cap_theirs = prepare(scalars, in_hbm(u_tilde), in_hbm(v_right))
    part_struct = struct((N_CAP, part, R), BF)
    own, s1, s2, s3 = kernel_call(
        cap_parts_body,
        (struct((N_CAP, part, R), F32), part_struct, part_struct, part_struct),
        1,
        2,
        name="cap_parts",
    )(scalars, cap_mine, to_core(cap_theirs))
    part1, part2, part3 = to_y(s1, 1), to_y(s2, 2), to_y(s3, 3)

    a_oth = to_core(after(leaf_inverse, own))
    vt_oth = to_core(after(vt, own))
    chip = kernel_call(
        chip_body, struct((C * rows, columns // C), BF), 1, 2, name="chip"
    )(scalars, after(mine, part1, vt_oth), other)
    before, behind = to_y(chip, 1), to_y(after(chip, part2, part3, a_oth), -1)
    def blocks(n, kind):
        return struct((n, part, R), kind)

    n1, n2, n3 = N_CAP - FIRST[1], N_CAP - FIRST[2], N_CAP - FIRST[3]
    cap_leaf, leaf_send, leaf_up = kernel_call(
        cap_leaf_body,
        (blocks(N_CAP, F32), blocks(N_CAP, BF), blocks(n1, BF)),
        0,
        4,
        name="cap_leaf",
    )(own, part1, part2, part3)
    low, cap_quad, quad_send, cap_quad_up = kernel_call(
        cap_x_body,
        (struct((2, FIRST[2], part, R), BF), blocks(n2, F32), blocks(n2, BF), blocks(n3, BF)),
        0,
        4,
        name="cap_x",
    )(cap_leaf, to_x(leaf_send, 1), to_x(leaf_up, 2), to_x(leaf_up, 3))
    mid, last = kernel_call(
        cap_z_body,
        (struct((2, FIRST[4] - FIRST[2], part, R), BF), blocks(1, F32)),
        0,
        4,
        name="cap_z",
    )(cap_quad, to_z(quad_send, 1), to_z(cap_quad_up, 2), to_z(cap_quad_up, 3))
    both = kernel_call(
        cap_both_body, struct((2 * N_CAP, part, R), BF), 0, 4, name="cap_both"
    )(low, mid, last, to_z(last, 4))
    top, bottom = kernel_call(
        halves_body, (part_shape, part_shape), 0, 2, name="halves"
    )(after(before, both), behind)
    far_top, far_bottom = to_y(top, 1), to_y(bottom, -1)
    places = jnp.stack([y, c, leaf_sizes[0]])
    along = [(y + d) & (Y - 1) for d in range(Y)]
    sum_own, sum_oth, far_own, far_oth = leaf(
        [along[0], along[3], along[1], along[2]],
        in_hbm(leaf_inverse),
        in_hbm(a_oth),
        [chip, before, behind],
    )
    both = after(both, top)
    cap_rows = kernel_call(
        cap_stack_body, struct((2 * N_CAP, half, R), BF), 1, 4, name="cap_stack"
    )(scalars, *gather_y(both))
    h, diag = kernel_call(
        elimination_body,
        (struct((N_H * R, 2 * R), BF), struct((LEVELS, 2, R, R), BF)),
        2,
        3,
        scratch=[pltpu.VMEM((2 * N_CAP, R, R), BF)],
        name="elimination",
        us=2.5,
    )(scalars, side, cap_rows, to_core(cap_rows), g)

    places = after(places, cap_rows)
    y_own, y_oth, *q = kernel_call(
        leaf_end_body,
        [struct((rows, columns // C), F32)] * 2 + [struct((LEVELS * R, R), BF)] * (Y - 1),
        1,
        8,
        name="leaf_end",
        us=4.0,
    )(places, far_own, far_oth, far_top, far_bottom, sum_own, sum_oth, vt, vt_oth)
    q_own = kernel_call(
        project_own_body, struct((LEVELS * R, R), BF), 1, 4, name="project_own", us=1.2
    )(places, y_own, y_oth, vt, vt_oth)
    y_other = to_core(y_oth)

    e, e_up = kernel_call(
        eliminate_body,
        (struct((LEVELS * R, R), BF), struct(((LEVELS - 1) * R, R), BF)),
        0,
        5,
        name="eliminate",
    )(q_own, to_y(q[0], 1), to_y(q[1], 2), to_y(q[2], 3), after(h, y_other))
    two = struct((2 * R, R), BF)
    r1, r2, r3 = to_x(e, 1), to_x(e_up, 2), to_x(e_up, 3)
    quad, quad_up = kernel_call(
        quad_body, (struct((3 * R, R), BF), struct((2 * R, R), BF)), 0, 4, name="quad"
    )(e, r1, r2, r3)
    z1, z2, z3 = to_z(quad, 1), to_z(quad_up, 2), to_z(quad_up, 3)
    t01 = kernel_call(
        lambda *refs: solve_two_body((0, 1), *refs), two, 1, 6, name="solve_0_1"
    )(side, diag, g, after(e, quad), r1, r2, r3)
    own4 = kernel_call(own4_body, struct((R, R), BF), 0, 4, name="own4")(
        after(quad, t01), z1, z2, z3
    )
    sib4 = to_z(own4, 4)
    t23 = kernel_call(
        lambda *refs: solve_two_body((2, 3), *refs), two, 1, 6, name="solve_2_3"
    )(side, diag, g, after(quad, own4), z1, z2, z3)
    t = kernel_call(solve_last_body, struct((LEVELS * R, R), BF), 1, 6, name="solve_4")(
        side, diag, g, own4, sib4, t01, t23
    )
    t_own = put_columns(y, gather_y(t))
    t_oth = to_core(t_own)
    return update(scalars, *bring(y_own, y_other, u_tilde), t_own, t_oth)


def solution(mesh):
    return jax.shard_map(
        shards,
        mesh=mesh,
        in_specs=(
            P(("partner", "row"), None),
            P(("partner", "row"), None),
            P("partner"),
            P(None, ("partner", "row"), None),
            P(None, ("partner", "row"), None),
            P(None, "partner", None, None),
        ),
        out_specs=P(("partner", "row"), None),
        check_vma=False,
    )
```

```python
import jax
import jax.numpy as jnp
from jax import lax
from jax.experimental import pallas as pl
from jax.experimental.pallas import tpu as pltpu
from jax.sharding import PartitionSpec as P

Z, X, Y, C = 8, 4, 4, 2
LEVELS = 5
R = 128
BF = jnp.bfloat16
F32 = jnp.float32
FIRST = (0, 5, 9, 12, 14)
N_CAP = 15
H_FIRST = (0, 4, 7, 9)
N_H = 10
VMEM_LIMIT = 16 * 1024 * 1024


def move(block, where):
    route = []
    for z in range(Z):
        for x in range(X):
            for y in range(Y):
                for c in range(C):
                    z1, x1, y1, c1 = where(z, x, y, c)
                    here = ((z * X + x) * Y + y) * C + c
                    there = ((z1 % Z * X + x1 % X) * Y + y1 % Y) * C + c1 % C
                    route.append((here, there))
    return lax.ppermute(block, ("partner", "row"), route)


def after(block, *others):
    return lax.optimization_barrier((block, *others))[0]


def in_hbm(block):
    return pltpu.with_memory_space_constraint(block, pltpu.HBM)


def to_core(block):
    return move(block, lambda z, x, y, c: (z, x, y, 1 - c))


def to_y(block, d):
    return move(block, lambda z, x, y, c: (z, x, y + d, c))


def to_x(block, mask):
    return move(block, lambda z, x, y, c: (z, x ^ mask, y, c))


def to_z(block, mask):
    return move(block, lambda z, x, y, c: (z ^ mask, x, y, c))


def dot(a, b):
    return jnp.dot(a, b, preferred_element_type=F32)


def split(a):
    upper = a.astype(BF)
    return upper, (a - upper.astype(F32)).astype(BF)


def dot_16_32(a, b):
    upper, lower = split(b)
    return dot(a, upper) + dot(a, lower)


def dot_32_32(a, b):
    a_upper, a_lower = split(a)
    b_upper, b_lower = split(b)
    return dot(a_upper, b_upper) + (dot(a_upper, b_lower) + dot(a_lower, b_upper))


def cost(microseconds):
    return pl.CostEstimate(
        flops=int(microseconds * 1.1e9), bytes_accessed=int(microseconds * 1e6), transcendentals=0
    )


def kernel_call(body, out_shape, n_scalar, n_in, scratch=(), name=None, us=None):
    smem = pl.BlockSpec(memory_space=pltpu.SMEM)
    vmem = pl.BlockSpec(memory_space=pltpu.VMEM)
    outs = out_shape if isinstance(out_shape, (tuple, list)) else (out_shape,)
    out_specs = [vmem] * len(outs)
    return pl.pallas_call(
        body,
        out_shape=out_shape,
        in_specs=[smem] * n_scalar + [vmem] * n_in,
        out_specs=out_specs if isinstance(out_shape, (tuple, list)) else vmem,
        scratch_shapes=list(scratch),
        compiler_params=pltpu.CompilerParams(vmem_limit_bytes=VMEM_LIMIT),
        cost_estimate=None if us is None else cost(us),
        name=name,
    )


def side_bits(upper, own, sib):
    return jnp.where(upper, sib, own), jnp.where(upper, own, sib)


def live_rhs_body(scalar_ref, rhs_hbm, mine_ref, theirs_ref, rhs_ref, sems):
    first, c = scalar_ref[0], scalar_ref[1]
    rows, half = mine_ref.shape
    tiles = sems.shape[0]
    tile = rows // tiles
    spans = [pl.ds(i * tile, tile) for i in range(tiles)]
    loads = [
        pltpu.make_async_copy(rhs_hbm.at[at], rhs_ref.at[at], sems.at[i])
        for i, at in enumerate(spans)
    ]
    for load in loads:
        load.start()
    iota = lax.broadcasted_iota(jnp.int32, (tile, 1), 0)
    for i, (load, at) in enumerate(zip(loads, spans)):
        load.wait()
        live = first + i * tile + iota < scalar_ref[2]
        for ref, core in ((mine_ref, c), (theirs_ref, 1 - c)):
            part = rhs_ref[at, pl.ds(pl.multiple_of(core * half, half), half)]
            ref[at, :] = jnp.where(live, part, 0.0).astype(BF)


def live_rhs(scalars, rhs):
    rows, columns = rhs.shape
    vmem = pl.BlockSpec(memory_space=pltpu.VMEM)
    out = jax.ShapeDtypeStruct((rows, columns // C), BF)
    return pl.pallas_call(
        live_rhs_body,
        out_shape=(out, out),
        in_specs=[pl.BlockSpec(memory_space=pltpu.SMEM), pl.BlockSpec(memory_space=pltpu.HBM)],
        out_specs=(vmem, vmem),
        scratch_shapes=[pltpu.VMEM(rhs.shape, F32), pltpu.SemaphoreType.DMA((4,))],
        compiler_params=pltpu.CompilerParams(vmem_limit_bytes=VMEM_LIMIT),
        cost_estimate=cost(2.1),
        name="live_rhs",
    )(scalars, rhs)


def chip_body(scalar_ref, mine_ref, other_ref, chip_ref):
    c = scalar_ref[1]
    rows = mine_ref.shape[0]
    for ref, core in ((mine_ref, c), (other_ref, 1 - c)):
        chip_ref[pl.ds(pl.multiple_of(core * rows, rows), rows), :] = ref[...]


def halves_body(before_ref, behind_ref, top_ref, bottom_ref):
    rows = top_ref.shape[0]
    top_ref[...] = before_ref[:rows]
    bottom_ref[...] = behind_ref[rows:]


def prepare_body(
    scalar_ref,
    u_hbm,
    v_hbm,
    vt_ref,
    mine_ref,
    theirs_ref,
    u_ref,
    v_ref,
    rows_ref,
    cap_ref,
    sems,
):
    loads = [
        pltpu.make_async_copy(u_hbm, u_ref, sems.at[0]),
        pltpu.make_async_copy(v_hbm, v_ref, sems.at[1]),
    ]
    for load in loads:
        load.start()
    rows = u_ref.shape[1]
    first, c = scalar_ref[0], scalar_ref[1]
    live = first + lax.broadcasted_iota(jnp.int32, (rows, 1), 0) < scalar_ref[2]
    loads[0].wait()
    for l in range(LEVELS):
        rows_ref[:, l * R : (l + 1) * R] = jnp.where(live, u_ref[l].astype(F32), 0.0).astype(BF)
    loads[1].wait()
    for l in range(LEVELS):
        vt_ref[l * R : (l + 1) * R, :] = v_ref[l].T
    for l in range(LEVELS):
        cap = dot(vt_ref[l * R : (l + 1) * R, :], rows_ref[:, : (l + 1) * R])
        for m in range(l + 1):
            cap_ref[FIRST[m] + l - m] = cap[:, m * R : (m + 1) * R]
    half = R // 2
    mine_ref[...] = cap_ref[:, pl.ds(pl.multiple_of(c * half, half), half), :]
    theirs_ref[...] = cap_ref[:, pl.ds(pl.multiple_of((1 - c) * half, half), half), :]


def prepare(scalars, u, v):
    levels, rows, _ = u.shape
    half = jax.ShapeDtypeStruct((N_CAP, R // 2, R), F32)
    hbm = pl.BlockSpec(memory_space=pltpu.HBM)
    vmem = pl.BlockSpec(memory_space=pltpu.VMEM)
    return pl.pallas_call(
        prepare_body,
        out_shape=(
            jax.ShapeDtypeStruct((levels * R, rows), BF),
            half,
            half,
        ),
        in_specs=[pl.BlockSpec(memory_space=pltpu.SMEM), hbm, hbm],
        out_specs=(vmem, vmem, vmem),
        scratch_shapes=[
            pltpu.VMEM(u.shape, BF),
            pltpu.VMEM(v.shape, BF),
            pltpu.VMEM((rows, levels * R), BF),
            pltpu.VMEM((N_CAP, R, R), F32),
            pltpu.SemaphoreType.DMA((2,)),
        ],
        compiler_params=pltpu.CompilerParams(vmem_limit_bytes=VMEM_LIMIT),
        name="prepare",
    )(scalars, u, v)


def cap_parts_body(scalar_ref, mine_ref, other_ref, own_ref, *send_refs):
    y = scalar_ref[3]
    part = own_ref.shape[1]

    def at(d):
        return pl.ds(pl.multiple_of(((y + d) & (Y - 1)) * part, part), part)

    own_ref[...] = mine_ref[:, at(0), :] + other_ref[:, at(0), :]
    for d, ref in enumerate(send_refs):
        ref[...] = (mine_ref[:, at(d + 1), :] + other_ref[:, at(d + 1), :]).astype(BF)


def cap_leaf_body(own_ref, r1_ref, r2_ref, r3_ref, leaf_ref, send_ref, upper_ref):
    leaf = (own_ref[...] + r1_ref[...].astype(F32)) + (
        r2_ref[...].astype(F32) + r3_ref[...].astype(F32)
    )
    leaf_ref[...] = leaf
    send_ref[...] = leaf.astype(BF)
    upper_ref[...] = leaf[FIRST[1] :].astype(BF)


def cap_x_body(leaf_ref, r1_ref, r2_ref, r3_ref, low_ref, quad_ref, send_ref, upper_ref):
    n0, n1 = FIRST[1], FIRST[2]
    low_ref[0, :n0] = leaf_ref[:n0].astype(BF)
    low_ref[1, :n0] = r1_ref[:n0]
    low_ref[0, n0:] = (leaf_ref[n0:n1] + r1_ref[n0:n1].astype(F32)).astype(BF)
    other = r2_ref[...].astype(F32) + r3_ref[...].astype(F32)
    low_ref[1, n0:] = other[: n1 - n0].astype(BF)
    quad = (leaf_ref[n1:] + r1_ref[n1:].astype(F32)) + other[n1 - n0 :]
    quad_ref[...] = quad
    send_ref[...] = quad.astype(BF)
    upper_ref[...] = quad[FIRST[3] - n1 :].astype(BF)


def cap_z_body(quad_ref, z1_ref, z2_ref, z3_ref, mid_ref, last_ref):
    n0, n1 = FIRST[3] - FIRST[2], FIRST[4] - FIRST[2]
    other = z2_ref[...].astype(F32) + z3_ref[...].astype(F32)
    mid_ref[0, :n0] = quad_ref[:n0].astype(BF)
    mid_ref[1, :n0] = z1_ref[:n0]
    mid_ref[0, n0:] = (quad_ref[n0:n1] + z1_ref[n0:n1].astype(F32)).astype(BF)
    mid_ref[1, n0:] = other[: n1 - n0].astype(BF)
    last_ref[...] = (quad_ref[n1:] + z1_ref[n1:].astype(F32)) + other[n1 - n0 :]


def cap_both_body(low_ref, mid_ref, own4_ref, sib4_ref, both_ref):
    for side, last_ref in enumerate((own4_ref, sib4_ref)):
        at = side * N_CAP
        both_ref[at : at + FIRST[2]] = low_ref[side]
        both_ref[at + FIRST[2] : at + FIRST[4]] = mid_ref[side]
        both_ref[at + FIRST[4]] = last_ref[0].astype(BF)


def cap_stack_body(scalar_ref, b0_ref, b1_ref, b2_ref, b3_ref, out_ref):
    part = b0_ref.shape[1]
    for d, ref in enumerate((b0_ref, b1_ref, b2_ref, b3_ref)):
        at = ((scalar_ref[3] + d) & (Y - 1)) * part
        out_ref[:, pl.ds(pl.multiple_of(at, part), part), :] = ref[...]


def elimination_body(scalar_ref, side_ref, mine_ref, other_ref, g_ref, h_ref, diag_ref, all_ref):
    c = scalar_ref[1]
    half = R // 2
    all_ref[:, pl.ds(pl.multiple_of(c * half, half), half), :] = mine_ref[...]
    all_ref[:, pl.ds(pl.multiple_of((1 - c) * half, half), half), :] = other_ref[...]
    rows = lax.broadcasted_iota(jnp.int32, (R, R), 0)
    cols = lax.broadcasted_iota(jnp.int32, (R, R), 1)
    eye = (rows == cols).astype(F32)
    for m in range(LEVELS):
        upper = side_ref[m] == 1
        first = FIRST[m]
        c0, c1 = side_bits(upper, all_ref[first], all_ref[N_CAP + first])
        diag_ref[m, 0] = c0
        diag_ref[m, 1] = c1
        if m == LEVELS - 1:
            break
        g = g_ref[m]
        g_hi, g_lo = split(g)
        gc0 = dot(g_hi, c0) + dot(g_lo, c0)
        m1 = jnp.where(upper, -gc0, g)
        m0 = jnp.where(upper, eye, 0.0) - dot_16_32(c1, m1)
        m0_hi, m0_lo = split(m0)
        m1_hi, m1_lo = split(m1)
        for l in range(m + 1, LEVELS):
            j = first + l - m
            a0, a1 = side_bits(upper, all_ref[j], all_ref[N_CAP + j])
            h = dot(a0, m0_hi) + dot(a0, m0_lo) + dot(a1, m1_hi) + dot(a1, m1_lo)
            hi, lo = split(h)
            at = (H_FIRST[m] + l - m - 1) * R
            h_ref[at : at + R, 0:R] = hi
            h_ref[at : at + R, R : 2 * R] = lo


def leaf_body(
    chip_ref, a0_hbm, a1_hbm, b0_ref, b1_ref, b2_ref, sum0, sum1, far0, far1, buffers, sems
):
    depth = b0_ref.shape[0]
    loads = []
    for k in range(Y):
        at = pl.ds(pl.multiple_of(chip_ref[k] * depth, depth), depth)
        for i, (a_hbm, far) in enumerate(((a0_hbm, far0), (a1_hbm, far1))):
            to = far if k == Y - 1 else buffers.at[k, i]
            loads.append(pltpu.make_async_copy(a_hbm.at[:, at], to, sems.at[k, i]))
    for load in loads:
        load.start()
    for k, block in enumerate((b0_ref, b1_ref, b2_ref)):
        for i, total in enumerate((sum0, sum1)):
            loads[2 * k + i].wait()
            new = dot(buffers[k, i], block[...])
            total[...] = new if k == 0 else total[...] + new
    for load in loads[2 * (Y - 1) :]:
        load.wait()


def leaf(chips, a_own, a_oth, blocks):
    rows = a_own.shape[0]
    depth, half = blocks[0].shape
    vmem = pl.BlockSpec(memory_space=pltpu.VMEM)
    hbm = pl.BlockSpec(memory_space=pltpu.HBM)
    out_shape = [jax.ShapeDtypeStruct((rows, half), F32)] * 2
    out_shape += [jax.ShapeDtypeStruct((rows, depth), BF)] * 2
    return pl.pallas_call(
        leaf_body,
        out_shape=out_shape,
        in_specs=[pl.BlockSpec(memory_space=pltpu.SMEM), hbm, hbm] + [vmem] * 3,
        out_specs=[vmem] * 4,
        scratch_shapes=[
            pltpu.VMEM((Y - 1, 2, rows, depth), BF),
            pltpu.SemaphoreType.DMA((Y, 2)),
        ],
        compiler_params=pltpu.CompilerParams(vmem_limit_bytes=VMEM_LIMIT),
        cost_estimate=cost(5.6),
        name="leaf",
    )(jnp.stack(chips), a_own, a_oth, *blocks)


def project(blocks, y_refs, v_refs, q_refs):
    q = None
    for y_ref, v_ref in zip(y_refs, v_refs):
        parts = []
        for block in blocks:
            at = pl.ds(pl.multiple_of((block & (Y - 1)) * R, R), R)
            parts.append(y_ref[:, at].astype(BF))
        new = dot(v_ref[...], parts[0] if len(parts) == 1 else jnp.concatenate(parts, axis=1))
        q = new if q is None else q + new
    for k, q_ref in enumerate(q_refs):
        q_ref[...] = q[:, k * R : (k + 1) * R].astype(BF)


def leaf_end_body(
    scalar_ref, a0_ref, a1_ref, top_ref, bottom_ref, sum0_ref, sum1_ref, va_ref, vb_ref, *out_refs
):
    y_refs, q_refs = out_refs[:2], out_refs[2:]
    rows = y_refs[0].shape[0]
    y, c, size = scalar_ref[0], scalar_ref[1], scalar_ref[2]
    iota = lax.broadcasted_iota(jnp.int32, (rows, 1), 0)
    far = jnp.concatenate([top_ref[...], bottom_ref[...]], axis=0)
    for a_ref, sum_ref, y_ref, core in zip(
        (a0_ref, a1_ref), (sum0_ref, sum1_ref), y_refs, (c, 1 - c)
    ):
        new = dot(a_ref[...], far)
        live = (y * C + core) * rows + iota < size
        y_ref[...] = jnp.where(live, sum_ref[...] + new, 0.0)
    project([y + d + 1 for d in range(len(q_refs))], y_refs, (va_ref, vb_ref), q_refs)


def project_own_body(place_ref, y0_ref, y1_ref, va_ref, vb_ref, q_ref):
    project([place_ref[0]], (y0_ref, y1_ref), (va_ref, vb_ref), [q_ref])


def eliminate_body(q0_ref, q1_ref, q2_ref, q3_ref, h_ref, e_ref, upper_ref):
    q = (q0_ref[...].astype(F32) + q1_ref[...].astype(F32)) + (
        q2_ref[...].astype(F32) + q3_ref[...].astype(F32)
    )
    for m in range(LEVELS):
        e = q[:R].astype(BF)
        e_ref[m * R : (m + 1) * R, :] = e
        if m > 0:
            upper_ref[(m - 1) * R : m * R, :] = e
        if m < LEVELS - 1:
            at, n = H_FIRST[m] * R, (LEVELS - 1 - m) * R
            q = q[R:] - dot(h_ref[at : at + n, :], jnp.concatenate([e, e], axis=0))


def solve(c0, c1, upper, own, sib, g):
    s0, s1 = side_bits(upper, own, sib)
    inner = s0 - dot_16_32(c0, s1)
    t1 = dot_32_32(g, inner)
    t0 = s1 - dot_16_32(c1, t1)
    return jnp.where(upper, t1, t0)


def solve_two_body(levels, side_ref, diag_ref, g_ref, a_ref, r1_ref, r2_ref, r3_ref, t_ref):
    low, high = levels
    one = slice(0, R)
    two = slice(R, 2 * R)
    t = solve(
        diag_ref[low, 0],
        diag_ref[low, 1],
        side_ref[low] == 1,
        a_ref[one].astype(F32),
        r1_ref[one].astype(F32),
        g_ref[low],
    )
    t_ref[one] = t.astype(BF)
    t = solve(
        diag_ref[high, 0],
        diag_ref[high, 1],
        side_ref[high] == 1,
        a_ref[two].astype(F32) + r1_ref[two].astype(F32),
        r2_ref[one].astype(F32) + r3_ref[one].astype(F32),
        g_ref[high],
    )
    t_ref[two] = t.astype(BF)


def quad_body(e_ref, r1_ref, r2_ref, r3_ref, quad_ref, upper_ref):
    two = slice(2 * R, 5 * R)
    quad = e_ref[two].astype(F32) + r1_ref[two].astype(F32)
    quad = quad + (r2_ref[R:].astype(F32) + r3_ref[R:].astype(F32))
    quad = quad.astype(BF)
    quad_ref[...] = quad
    upper_ref[...] = quad[R:]


def own4_body(quad_ref, z1_ref, z2_ref, z3_ref, own_ref):
    own = quad_ref[2 * R :].astype(F32) + z1_ref[2 * R :].astype(F32)
    own_ref[...] = (own + (z2_ref[R:].astype(F32) + z3_ref[R:].astype(F32))).astype(BF)


def solve_last_body(side_ref, diag_ref, g_ref, a_ref, r_ref, t01_ref, t23_ref, t_ref):
    last = LEVELS - 1
    t = solve(
        diag_ref[last, 0],
        diag_ref[last, 1],
        side_ref[last] == 1,
        a_ref[...].astype(F32),
        r_ref[...].astype(F32),
        g_ref[last],
    )
    t_ref[: 2 * R] = t01_ref[...]
    t_ref[2 * R : 4 * R] = t23_ref[...]
    t_ref[4 * R :] = t.astype(BF)


def columns_body(y_ref, b0_ref, b1_ref, b2_ref, b3_ref, out_ref):
    for d, ref in enumerate((b0_ref, b1_ref, b2_ref, b3_ref)):
        at = ((y_ref[0] + d) & (Y - 1)) * R
        out_ref[:, pl.ds(pl.multiple_of(at, R), R)] = ref[...]


def gather_y(block):
    return [block, to_y(block, -1), to_y(block, 2), to_y(block, 1)]


def put_columns(y, blocks):
    out = jax.ShapeDtypeStruct((blocks[0].shape[0], Y * R), BF)
    return kernel_call(columns_body, out, 1, Y, name="columns")(y[None], *blocks)


def bring_body(*refs):
    n = (len(refs) - 1) // 2
    sems = refs[-1]
    copies = [
        pltpu.make_async_copy(refs[i], refs[n + i], sems.at[i]) for i in range(n)
    ]
    for copy in copies:
        copy.start()
    for copy in copies:
        copy.wait()


def bring(*arrays):
    n = len(arrays)
    size = sum(a.size * a.dtype.itemsize for a in arrays)
    return pl.pallas_call(
        bring_body,
        out_shape=[jax.ShapeDtypeStruct(a.shape, a.dtype) for a in arrays],
        in_specs=[pl.BlockSpec(memory_space=pltpu.HBM)] * n,
        out_specs=[pl.BlockSpec(memory_space=pltpu.VMEM)] * n,
        scratch_shapes=[pltpu.SemaphoreType.DMA((n,))],
        compiler_params=pltpu.CompilerParams(vmem_limit_bytes=VMEM_LIMIT),
        cost_estimate=pl.CostEstimate(flops=0, bytes_accessed=2 * size, transcendentals=0),
        name="bring",
    )(*[in_hbm(a) for a in arrays])


def update_body(scalar_ref, y0_ref, y1_ref, u_ref, t0_ref, t1_ref, out_hbm, held, sems):
    rows, half = y0_ref.shape
    tiles = sems.shape[0]
    tile = rows // tiles
    first, c, size = scalar_ref[0], scalar_ref[1], scalar_ref[2]
    iota = lax.broadcasted_iota(jnp.int32, (tile, 1), 0)
    copies = []
    for i in range(tiles):
        at_row = pl.ds(i * tile, tile)
        u = jnp.concatenate([u_ref[l, at_row, :] for l in range(LEVELS)], axis=1)
        live = first + i * tile + iota < size
        for y_ref, t_ref, core in ((y0_ref, t0_ref, c), (y1_ref, t1_ref, 1 - c)):
            at = pl.ds(pl.multiple_of(core * half, half), half)
            held[at_row, at] = y_ref[at_row, :] - jnp.where(live, dot(u, t_ref[...]), 0.0)
        copy = pltpu.make_async_copy(held.at[at_row], out_hbm.at[at_row], sems.at[i])
        copy.start()
        copies.append(copy)
    for copy in copies:
        copy.wait()


def update(scalars, y_own, y_oth, u, t_own, t_oth):
    rows, half = y_own.shape
    vmem = pl.BlockSpec(memory_space=pltpu.VMEM)
    return pl.pallas_call(
        update_body,
        out_shape=jax.ShapeDtypeStruct((rows, 2 * half), F32),
        in_specs=[pl.BlockSpec(memory_space=pltpu.SMEM)] + [vmem] * 5,
        out_specs=pl.BlockSpec(memory_space=pl.ANY),
        scratch_shapes=[pltpu.VMEM((rows, 2 * half), F32), pltpu.SemaphoreType.DMA((4,))],
        compiler_params=pltpu.CompilerParams(vmem_limit_bytes=VMEM_LIMIT),
        name="update",
    )(scalars, y_own, y_oth, u, t_own, t_oth)


def shards(rhs, leaf_inverse, leaf_sizes, u_tilde, v_right, cap_factor):
    rows, columns = rhs.shape
    row = lax.axis_index("row").astype(jnp.int32)
    partner = lax.axis_index("partner").astype(jnp.int32)
    y, c = row >> 1, row & 1
    side = (partner >> jnp.arange(LEVELS, dtype=jnp.int32)) & 1
    scalars = jnp.stack([row * rows, c, leaf_sizes[0], y])
    g = cap_factor[:, 0]
    struct = jax.ShapeDtypeStruct

    part_shape = struct((rows, columns // C), BF)
    mine, theirs = live_rhs(scalars, in_hbm(rhs))
    other = to_core(theirs)

    half, part = R // 2, R // C // Y
    vt, cap_mine, cap_theirs = prepare(scalars, in_hbm(u_tilde), in_hbm(v_right))
    part_struct = struct((N_CAP, part, R), BF)
    own, s1, s2, s3 = kernel_call(
        cap_parts_body,
        (struct((N_CAP, part, R), F32), part_struct, part_struct, part_struct),
        1,
        2,
        name="cap_parts",
    )(scalars, cap_mine, to_core(cap_theirs))
    part1, part2, part3 = to_y(s1, 1), to_y(s2, 2), to_y(s3, 3)

    a_oth = to_core(after(leaf_inverse, own))
    vt_oth = to_core(after(vt, own))
    chip = kernel_call(
        chip_body, struct((C * rows, columns // C), BF), 1, 2, name="chip"
    )(scalars, after(mine, part1, vt_oth), other)
    before, behind = to_y(chip, 1), to_y(after(chip, part2, part3, a_oth), -1)
    def blocks(n, kind):
        return struct((n, part, R), kind)

    n1, n2, n3 = N_CAP - FIRST[1], N_CAP - FIRST[2], N_CAP - FIRST[3]
    cap_leaf, leaf_send, leaf_up = kernel_call(
        cap_leaf_body,
        (blocks(N_CAP, F32), blocks(N_CAP, BF), blocks(n1, BF)),
        0,
        4,
        name="cap_leaf",
    )(own, part1, part2, part3)
    low, cap_quad, quad_send, cap_quad_up = kernel_call(
        cap_x_body,
        (struct((2, FIRST[2], part, R), BF), blocks(n2, F32), blocks(n2, BF), blocks(n3, BF)),
        0,
        4,
        name="cap_x",
    )(cap_leaf, to_x(leaf_send, 1), to_x(leaf_up, 2), to_x(leaf_up, 3))
    mid, last = kernel_call(
        cap_z_body,
        (struct((2, FIRST[4] - FIRST[2], part, R), BF), blocks(1, F32)),
        0,
        4,
        name="cap_z",
    )(cap_quad, to_z(quad_send, 1), to_z(cap_quad_up, 2), to_z(cap_quad_up, 3))
    both = kernel_call(
        cap_both_body, struct((2 * N_CAP, part, R), BF), 0, 4, name="cap_both"
    )(low, mid, last, to_z(last, 4))
    top, bottom = kernel_call(
        halves_body, (part_shape, part_shape), 0, 2, name="halves"
    )(after(before, both), behind)
    far_top, far_bottom = to_y(top, 1), to_y(bottom, -1)
    places = jnp.stack([y, c, leaf_sizes[0]])
    along = [(y + d) & (Y - 1) for d in range(Y)]
    sum_own, sum_oth, far_own, far_oth = leaf(
        [along[0], along[3], along[1], along[2]],
        in_hbm(leaf_inverse),
        in_hbm(a_oth),
        [chip, before, behind],
    )
    both = after(both, top)
    cap_rows = kernel_call(
        cap_stack_body, struct((2 * N_CAP, half, R), BF), 1, 4, name="cap_stack"
    )(scalars, *gather_y(both))
    h, diag = kernel_call(
        elimination_body,
        (struct((N_H * R, 2 * R), BF), struct((LEVELS, 2, R, R), BF)),
        2,
        3,
        scratch=[pltpu.VMEM((2 * N_CAP, R, R), BF)],
        name="elimination",
        us=2.5,
    )(scalars, side, cap_rows, to_core(cap_rows), g)

    places = after(places, cap_rows)
    y_own, y_oth, *q = kernel_call(
        leaf_end_body,
        [struct((rows, columns // C), F32)] * 2 + [struct((LEVELS * R, R), BF)] * (Y - 1),
        1,
        8,
        name="leaf_end",
        us=4.0,
    )(places, far_own, far_oth, far_top, far_bottom, sum_own, sum_oth, vt, vt_oth)
    q_own = kernel_call(
        project_own_body, struct((LEVELS * R, R), BF), 1, 4, name="project_own", us=1.2
    )(places, y_own, y_oth, vt, vt_oth)
    y_other = to_core(y_oth)

    e, e_up = kernel_call(
        eliminate_body,
        (struct((LEVELS * R, R), BF), struct(((LEVELS - 1) * R, R), BF)),
        0,
        5,
        name="eliminate",
    )(q_own, to_y(q[0], 1), to_y(q[1], 2), to_y(q[2], 3), after(h, y_other))
    two = struct((2 * R, R), BF)
    r1, r2, r3 = to_x(e, 1), to_x(e_up, 2), to_x(e_up, 3)
    quad, quad_up = kernel_call(
        quad_body, (struct((3 * R, R), BF), struct((2 * R, R), BF)), 0, 4, name="quad"
    )(e, r1, r2, r3)
    z1, z2, z3 = to_z(quad, 1), to_z(quad_up, 2), to_z(quad_up, 3)
    t01 = kernel_call(
        lambda *refs: solve_two_body((0, 1), *refs), two, 1, 6, name="solve_0_1"
    )(side, diag, g, after(e, quad), r1, r2, r3)
    own4 = kernel_call(own4_body, struct((R, R), BF), 0, 4, name="own4")(
        after(quad, t01), z1, z2, z3
    )
    sib4 = to_z(own4, 4)
    t23 = kernel_call(
        lambda *refs: solve_two_body((2, 3), *refs), two, 1, 6, name="solve_2_3"
    )(side, diag, g, after(quad, own4), z1, z2, z3)
    t = kernel_call(solve_last_body, struct((LEVELS * R, R), BF), 1, 6, name="solve_4")(
        side, diag, g, own4, sib4, t01, t23
    )
    t_own = put_columns(y, gather_y(t))
    t_oth = to_core(t_own)
    return update(scalars, *bring(y_own, y_other, u_tilde), t_own, t_oth)


def solution(mesh):
    return jax.shard_map(
        shards,
        mesh=mesh,
        in_specs=(
            P(("partner", "row"), None),
            P(("partner", "row"), None),
            P("partner"),
            P(None, ("partner", "row"), None),
            P(None, ("partner", "row"), None),
            P(None, "partner", None, None),
        ),
        out_specs=P(("partner", "row"), None),
        check_vma=False,
    )
```
